32 devices in a mesh: expert: 8 (over z, x), hidden: 4 (over y, core).
Axes of the slice: x: 2, y: 2, z: 4, core: 2. Of those that a mesh axis runs over, the one named last changes fastest.
Arguments:
- images: bfloat16 [224, 144, 512], P(('expert', 'hidden')), may hold values from -6 to 6
- lengths: int32 [224], P(('expert', 'hidden')), may hold values from 49 to 144, as said below
- priority: int32 [32, 1008], P(('expert', 'hidden')), may hold values from 0 to 1007, each once within a row
- top_experts: int32 [224, 144, 2], P(('expert', 'hidden')), may hold values from 0 to 7, all different within a row
- out_grad: bfloat16 [224, 144, 512], P(('expert', 'hidden')), may hold values from -6 to 6
- first_gain: float32 [512], replicated, may hold values from 0.5 to 1.5
- first_shift: float32 [512], replicated, may hold values from -1 to 1
- w_query: bfloat16 [512, 512], replicated, may hold values from -0.375 to 0.375
- w_key: bfloat16 [512, 512], replicated, may hold values from -0.25 to 0.25
- w_value: bfloat16 [512, 512], replicated, may hold values from -0.25 to 0.25
- w_output: bfloat16 [512, 512], replicated, may hold values from -0.75 to 0.75
- second_gain: float32 [512], replicated, may hold values from 0.5 to 1.5
- second_shift: float32 [512], replicated, may hold values from -0.5 to 0.5
- w_router: bfloat16 [512, 8], replicated, may hold values from -0.1875 to 0.1875
- w_expert_in: bfloat16 [8, 512, 2048], P('expert', None, 'hidden'), may hold values from -0.25 to 0.25
- w_expert_out: bfloat16 [8, 2048, 512], P('expert', 'hidden'), may hold values from -2 to 2
Outputs:
- block_out: bfloat16 [224, 144, 512], P(('expert', 'hidden'))
- grad_images: float32 [224, 144, 512], P(('expert', 'hidden'))
- grad_first_gain: float32 [512], replicated
- grad_first_shift: float32 [512], replicated
- grad_w_query: float32 [512, 512], replicated
- grad_w_key: float32 [512, 512], replicated
- grad_w_value: float32 [512, 512], replicated
- grad_w_output: float32 [512, 512], replicated
- grad_second_gain: float32 [512], replicated
- grad_second_shift: float32 [512], replicated
- grad_w_router: float32 [512, 8], replicated
- grad_w_expert_in: float32 [8, 512, 2048], P('expert', None, 'hidden')
- grad_w_expert_out: float32 [8, 2048, 512], P('expert', 'hidden')
The draws below stay inside these ranges and needn't reach their ends.
Inputs may be any that keep to these rules, and one draw needn't show every extreme that they name: `lengths`: each image has either 49 or 144 valid patches, the first ones; the rest are padding. `priority`: each row is an ordering of the 1008 token slots of one routing group. `top_experts`: the two experts of a token differ; choices of padding tokens are ignored.
All inputs are finite; a program needn't handle non-finite values.
Results may differ from the reference program's by a relative error of at most 0.015.
Values may be sent and summed in bfloat16 or wider, within the bound.
No kernel may reach another device: no remote copies, remote signals or barrier semaphores. Data moves between devices by JAX's collectives and lax.ppermute only.
A program may use at most 192 MiB of HBM per device.

```python
import jax
import jax.numpy as jnp
from jax import lax

D = 512
HEADS = 8
HEAD_DIM = 64
FF = 2048
TOPK = 2
PATCHES = 144
SHORT = 49
IMG_DEV = 7
GROUPS = 32
IMAGES = 224
TOK_DEV = 1008
EXPERTS = 8
CAP = 265


def draw_lengths(key, part):
    key = jax.random.fold_in(key, 11)
    coins = jax.random.randint(key, (IMAGES,), 0, 2)
    return jnp.where(coins == 1, PATCHES, SHORT).astype(jnp.int32)


def level_of(own_key, extent, cuts, least, high):
    def one(axis_at, parts):
        steps = jax.random.uniform(jax.random.fold_in(jax.random.fold_in(own_key, 6), axis_at), (parts,), jnp.float32, least / len(cuts), high / len(cuts))
        return jnp.repeat(jnp.exp(steps), extent[axis_at] // parts).reshape((-1,) + (1,) * (len(extent) - axis_at - 1))

    factor_of = one(*cuts[0])
    for cut in cuts[1:]:
        factor_of = factor_of * one(*cut)
    return factor_of


def picks_of(key, rows, number_of, top, lift):
    order = jax.random.permutation(jax.random.fold_in(key, 1), number_of)
    boost = order
    for power in range(3):
        boost = boost * boost // number_of
    boost = boost * lift // number_of
    tickets = jax.random.randint(jax.random.fold_in(key, 2), (rows, number_of), 0, 4096) + boost
    fixed_rows = jax.random.permutation(jax.random.fold_in(key, 3), rows)[jnp.arange(number_of) % rows]
    tickets = jnp.where(jnp.arange(rows)[:, None] == fixed_rows[None, :], 1 << 14, tickets)
    score = tickets * number_of + jnp.arange(number_of)
    return lax.top_k(score.astype(jnp.int32), top)[1].astype(jnp.int32)


def scatter_about(stream_key, shape, width, most, shards=(), kind=jnp.bfloat16):
    level = level_of(stream_key, shape, shards, -0.22, 0.18) if shards else 1.0
    array = jax.random.normal(stream_key, shape, jnp.float32) * width * level
    return jnp.minimum(jnp.maximum(array, -most), most).astype(kind)


def setup_inputs(seed: int = 0) -> dict:
    key_list = jax.random.split(jax.random.key(seed), 17)
    images = scatter_about(key_list[0], (IMAGES, PATCHES, D), 1.0, 6.0, ((0, 32),))
    lengths = draw_lengths(jax.random.fold_in(key_list[16], 71), 0)
    priority = jax.vmap(lambda own: jax.random.permutation(own, TOK_DEV))(jax.random.split(key_list[2], GROUPS)).reshape((GROUPS, TOK_DEV)).astype(jnp.int32)
    top_experts = picks_of(key_list[3], IMAGES * PATCHES, EXPERTS, TOPK, 2048).reshape((IMAGES, PATCHES, TOPK))
    out_grad = scatter_about(key_list[4], (IMAGES, PATCHES, D), 1.0, 6.0, ((0, 32),))
    first_gain = jnp.clip(1.0 + 0.1 * jax.random.normal(key_list[5], (D,), jnp.float32), 0.5, 1.5)
    first_shift = scatter_about(key_list[6], (D,), 0.2, 1.0, (), jnp.float32)
    w_query = scatter_about(key_list[7], (D, D), (D // 2) ** -0.5, 0.375)
    w_key = scatter_about(key_list[8], (D, D), D ** -0.5, 0.25)
    w_value = scatter_about(key_list[9], (D, D), D ** -0.5, 0.25)
    w_output = scatter_about(key_list[10], (D, D), (D // 8) ** -0.5, 0.75)
    second_gain = jnp.clip(1.0 + 0.1 * jax.random.normal(key_list[11], (D,), jnp.float32), 0.5, 1.5)
    second_shift = scatter_about(key_list[12], (D,), 0.1, 0.5, (), jnp.float32)
    w_router = scatter_about(key_list[13], (D, EXPERTS), (2 * D) ** -0.5, 0.1875)
    w_expert_in = scatter_about(key_list[14], (EXPERTS, D, FF), D ** -0.5, 0.25, ((0, 8), (2, 4)))
    w_expert_out = scatter_about(key_list[15], (EXPERTS, FF, D), 8 ** -0.5, 2.0, ((0, 8), (1, 4)))
    return dict(images=images, lengths=lengths, priority=priority, top_experts=top_experts, out_grad=out_grad, first_gain=first_gain, first_shift=first_shift, w_query=w_query, w_key=w_key, w_value=w_value, w_output=w_output, second_gain=second_gain, second_shift=second_shift, w_router=w_router, w_expert_in=w_expert_in, w_expert_out=w_expert_out)


HIGHEST = lax.Precision.HIGHEST
EPSILON = 1e-06
NEGATIVE = -1e+30

@jax.custom_vjp
def low(v):
    return lax.optimization_barrier(v.astype(jnp.bfloat16)).astype(jnp.float32)

@jax.custom_vjp
def low_back(v):
    return v

def low_keep(v):
    return (low(v), None)

def low_pass(kept, grad):
    return (grad,)

def back_keep(v):
    return (v, None)

def back_low(kept, grad):
    return (low(grad),)
low.defvjp(low_keep, low_pass)
low_back.defvjp(back_keep, back_low)

def layer_norm(values, scaling, offset):
    average = lax.optimization_barrier(jnp.mean(values, axis=-1, keepdims=True))
    centred = values - average
    variance = lax.optimization_barrier(jnp.mean(centred * centred, axis=-1, keepdims=True))
    return centred * lax.rsqrt(variance + EPSILON) * scaling + offset

def slot_targets(selected, present, ranking, expert_count, capacity):
    rows_count, top_count = selected.shape
    ranked = selected[ranking]
    ranked_present = present[ranking]
    flattened = ranked.T.reshape(-1).astype(jnp.int32)
    active = jnp.tile(ranked_present, top_count)
    labels = jnp.arange(expert_count, dtype=jnp.int32)
    onehot = ((flattened[:, None] == labels[None, :]) & active[:, None]).astype(jnp.int32)
    earlier = jnp.cumsum(onehot, axis=0, dtype=jnp.int32) - onehot
    position = lax.optimization_barrier(jnp.sum(earlier * onehot, axis=1, dtype=jnp.int32))
    retained = active & (position < capacity)
    target = jnp.where(retained, flattened * capacity + position, expert_count * capacity).astype(jnp.int32)
    target = target.reshape(top_count, rows_count).T
    inverse = jnp.zeros((rows_count,), jnp.int32).at[ranking].set(jnp.arange(rows_count, dtype=jnp.int32))
    return target[inverse]

def reference(images, lengths, priority, top_experts, out_grad, first_gain, first_shift, w_query, w_key, w_value, w_output, second_gain, second_shift, w_router, w_expert_in, w_expert_out):
    present = jnp.arange(PATCHES, dtype=jnp.int32)[None, :] < lengths[:, None]
    selected = top_experts.reshape(GROUPS, TOK_DEV, TOPK).astype(jnp.int32)
    targets = jax.vmap(lambda sel, pres, rank: slot_targets(sel, pres, rank, EXPERTS, CAP))(selected, present.reshape(GROUPS, TOK_DEV), priority.astype(jnp.int32))
    scaling = HEAD_DIM ** (-0.5)

    def forward(tokens, gain_one, shift_one, query_w, key_w, value_w, output_w, gain_two, shift_two, router_w, expert_first, expert_second):

        def front(block_pair):
            group_tokens, group_mask = block_pair
            normed = low(layer_norm(group_tokens, gain_one, shift_one))
            split_shape = (IMG_DEV, PATCHES, HEADS, HEAD_DIM)
            queries = low(low_back(jnp.dot(normed, query_w, precision=HIGHEST))).reshape(split_shape)
            key_rows = low(low_back(jnp.dot(normed, key_w, precision=HIGHEST))).reshape(split_shape)
            values = low(low_back(jnp.dot(normed, value_w, precision=HIGHEST))).reshape(split_shape)
            scores = low_back(jnp.einsum('iphd,iqhd->ihpq', queries, key_rows, precision=HIGHEST) * scaling)
            scores = jnp.where(group_mask[:, None, None, :], scores, NEGATIVE)
            attn_probs = low(jax.nn.softmax(scores, axis=-1))
            mixed = jnp.einsum('ihpq,iqhd->iphd', attn_probs, values, precision=HIGHEST).reshape(IMG_DEV, PATCHES, D)
            mixed = low(low_back(mixed))
            residual = group_tokens + low_back(jnp.dot(mixed, output_w, precision=HIGHEST))
            normed_two = low(layer_norm(residual, gain_two, shift_two))
            return (residual, normed_two)
        residual, normed_two = lax.map(jax.checkpoint(front), (tokens.reshape(GROUPS, IMG_DEV, PATCHES, D), present.reshape(GROUPS, IMG_DEV, PATCHES)))
        residual = residual.reshape(GROUPS, TOK_DEV, D)
        normed_two = normed_two.reshape(GROUPS, TOK_DEV, D)
        logits = low_back(jnp.dot(normed_two, router_w, precision=HIGHEST))
        router = jax.nn.softmax(logits, axis=-1)
        gate_values = jnp.take_along_axis(router, selected, axis=2)

        def dispatch(normed_group, target_group):
            buffer = jnp.zeros((EXPERTS * CAP + 1, D), jnp.float32)
            for column in range(TOPK):
                buffer = buffer.at[target_group[:, column]].add(normed_group)
            return buffer[:EXPERTS * CAP]
        slots = low_back(jax.vmap(dispatch)(normed_two, targets))
        slots = slots.reshape(GROUPS, EXPERTS, CAP, D).transpose(1, 0, 2, 3).reshape(EXPERTS, GROUPS * CAP, D)

        def expert(block_triple):
            rows, weight_first, weight_second = block_triple
            hidden_pre = low_back(jnp.dot(rows, weight_first, precision=HIGHEST))
            activated = low(jax.nn.gelu(hidden_pre, approximate=False))
            return low(low_back(jnp.dot(activated, weight_second, precision=HIGHEST)))
        results = lax.map(jax.checkpoint(expert), (slots, expert_first, expert_second))
        results = results.reshape(EXPERTS, GROUPS, CAP, D).transpose(1, 0, 2, 3).reshape(GROUPS, EXPERTS * CAP, D)

        def combine(result_group, target_group, gate_group):
            extended = jnp.concatenate([result_group, jnp.zeros((1, D), jnp.float32)])
            accumulated = jnp.zeros((TOK_DEV, D), jnp.float32)
            for column in range(TOPK):
                accumulated = accumulated + gate_group[:, column:column + 1] * extended[target_group[:, column]]
            return accumulated
        moe_part = jax.vmap(combine)(results, targets, gate_values)
        return (residual + moe_part).reshape(IMAGES, PATCHES, D)
    floats = tuple((array_in.astype(jnp.float32) for array_in in (images, first_gain, first_shift, w_query, w_key, w_value, w_output, second_gain, second_shift, w_router, w_expert_in, w_expert_out)))
    result, backward = jax.vjp(forward, *floats)
    gradients = backward(out_grad.astype(jnp.float32))
    return (result.astype(jnp.bfloat16), gradients[0], gradients[1], gradients[2], gradients[3], gradients[4], gradients[5], gradients[6], gradients[7], gradients[8], gradients[9], gradients[10], gradients[11])
```

```python
import jax
import jax.numpy as jnp
from jax import lax
from jax.sharding import PartitionSpec as P

HEADS = 8
TOPK = 2
EPSILON = 1e-06
NEGATIVE = -1e30
BF = jnp.bfloat16
F32 = jnp.float32


def swap(value, axes, size, flip):
    return lax.ppermute(value, axes, [(i, i ^ flip) for i in range(size)])


def bits_of(size):
    count = size.bit_length() - 1
    assert size == 1 << count
    return range(count)


def reduce_scatter(parts, axes, size):
    index = lax.axis_index(axes)
    for bit in bits_of(size):
        pairs = parts.reshape((parts.shape[0] // 2, 2) + parts.shape[1:])
        odd = ((index >> bit) & 1) == 1
        mine = jnp.where(odd, pairs[:, 1], pairs[:, 0])
        other = jnp.where(odd, pairs[:, 0], pairs[:, 1]).astype(BF)
        parts = mine + swap(other, axes, size, 1 << bit).astype(F32)
    return parts[0]


def all_gather(part, axes, size):
    index = lax.axis_index(axes)
    parts = part[None]
    for bit in reversed(bits_of(size)):
        odd = ((index >> bit) & 1) == 1
        came = swap(parts, axes, size, 1 << bit)
        pairs = jnp.where(odd, jnp.stack([came, parts], 1), jnp.stack([parts, came], 1))
        parts = pairs.reshape((-1,) + part.shape)
    return parts


def all_sum(value, axes, size):
    for bit in bits_of(size):
        value = value + swap(value, axes, size, 1 << bit)
    return value


def exchange(blocks, axes, size):
    index = lax.axis_index(axes)
    taken = []
    for flip in range(size):
        block = lax.dynamic_index_in_dim(blocks, index ^ flip, 0, keepdims=False)
        taken.append(block if flip == 0 else swap(block, axes, size, flip))
    return taken


def exchange_back(block_list, axes, size):
    index = lax.axis_index(axes)
    came = jnp.stack(
        [b if s == 0 else swap(b, axes, size, s) for s, b in enumerate(block_list)]
    )
    order = index ^ jnp.arange(size, dtype=jnp.int32)
    return came[order]


def layer_norm(values, scaling, offset):
    average = jnp.mean(values, axis=-1, keepdims=True)
    centred = values - average
    variance = jnp.mean(centred * centred, axis=-1, keepdims=True)
    return centred * lax.rsqrt(variance + EPSILON) * scaling + offset


def exact_gelu(values):
    return jax.nn.gelu(values, approximate=False)


def gate_lookup(logits, selected):
    chosen = selected[:, :, None] == jnp.arange(logits.shape[1], dtype=jnp.int32)
    router = jax.nn.softmax(logits, axis=-1)
    return jnp.sum(jnp.where(chosen, router[:, None, :], 0.0), axis=-1)


def slot_targets(selected, present, ranking, expert_count, capacity, stride):
    rows_count, top_count = selected.shape
    ranked = selected[ranking]
    ranked_present = present[ranking]
    flattened = ranked.T.reshape(-1)
    active = jnp.tile(ranked_present, top_count)
    labels = jnp.arange(expert_count, dtype=jnp.int32)
    onehot = ((flattened[:, None] == labels[None, :]) & active[:, None]).astype(jnp.int32)
    earlier = jnp.cumsum(onehot, axis=0, dtype=jnp.int32) - onehot
    position = jnp.sum(earlier * onehot, axis=1, dtype=jnp.int32)
    retained = active & (position < capacity)
    target = jnp.where(retained, flattened * stride + position, expert_count * stride)
    target = target.reshape(top_count, rows_count).T
    inverse = (
        jnp.zeros((rows_count,), jnp.int32).at[ranking].set(jnp.arange(rows_count, dtype=jnp.int32))
    )
    return target[inverse]


def mm(spec, left, right):
    return jnp.einsum(spec, left, right, preferred_element_type=F32)


def make_on_device(experts, hidden):
    def on_device(
        images,
        lengths,
        priority,
        top_experts,
        out_grad,
        first_gain,
        first_shift,
        w_query,
        w_key,
        w_value,
        w_output,
        second_gain,
        second_shift,
        w_router,
        w_expert_in,
        w_expert_out,
    ):
        world = ("expert", "hidden")
        image_count, patch_count, width = images.shape
        rows = image_count * patch_count
        head_size = width // HEADS
        scaling = head_size ** (-0.5)
        capacity = (21 * rows * TOPK + 20 * experts - 1) // (20 * experts)
        stride = (capacity + 15) // 16 * 16
        slots = experts * stride
        split_shape = (image_count, patch_count, HEADS, head_size)

        units = w_expert_in.shape[2]
        own = jnp.concatenate([w_expert_in[0].reshape(units, width), w_expert_out[0]])
        whole = all_gather(own, "hidden", hidden)
        weight_in = whole[:, :units].reshape(hidden, width, units)
        weight_out = whole[:, units:]

        present = jnp.arange(patch_count, dtype=jnp.int32)[None, :] < lengths[:, None]
        selected = top_experts.reshape(rows, TOPK)
        target = slot_targets(selected, present.reshape(rows), priority[0], experts, capacity, stride)
        slot_at = jnp.arange(slots, dtype=jnp.int32)
        chosen = [target[:, j : j + 1] == slot_at[None, :] for j in range(TOPK)]
        low_chosen = [c.astype(BF) for c in chosen]
        either = low_chosen[0] + low_chosen[1]

        cot_low = out_grad.reshape(rows, width)
        cot_slots = mm("ts,td->sd", either, cot_low).astype(BF).reshape(experts, stride, width)
        cot_in = exchange(cot_slots, "expert", experts)

        tokens = images.astype(F32).reshape(rows, width)
        normed_full, norm_one_back = jax.vjp(layer_norm, tokens, first_gain, first_shift)
        normed_low = normed_full.astype(BF)

        def project(matrix):
            return mm("td,de->te", normed_low, matrix).astype(BF).reshape(split_shape)

        queries = project(w_query)
        key_rows = project(w_key)
        values = project(w_value)
        key_mask = present[:, None, None, :]

        def score_block():
            raw_scores = mm("iphd,iqhd->ihpq", queries, key_rows) * scaling
            return jnp.where(key_mask, raw_scores, NEGATIVE)

        scores = score_block()
        row_max = jnp.max(scores, axis=-1, keepdims=True)
        exponent = jnp.exp(scores - row_max)
        denominator = jnp.sum(exponent, axis=-1, keepdims=True)
        attn_probs = exponent / denominator
        log_total = row_max + jnp.log(denominator)
        probs_low = attn_probs.astype(BF)
        mixed_heads = mm("ihpq,iqhd->iphd", probs_low, values).astype(BF).reshape(rows, width)
        residual = tokens + mm("td,de->te", mixed_heads, w_output)
        normed_two, norm_two_back = jax.vjp(layer_norm, residual, second_gain, second_shift)
        routed_low = normed_two.astype(BF)
        logits = mm("td,de->te", routed_low, w_router)
        gate_values, gate_back = jax.vjp(lambda v: gate_lookup(v, selected), logits)

        send_rows = mm("ts,td->sd", either, routed_low).astype(BF).reshape(experts, stride, width)
        gate_slots = sum(
            jnp.sum(jnp.where(chosen[j], gate_values[:, j : j + 1], 0.0), axis=0)
            for j in range(TOPK)
        ).reshape(experts, stride)
        rows_in = exchange(send_rows, "expert", experts)
        gates_in = exchange(gate_slots, "expert", experts)

        row_block = jnp.concatenate(rows_in)
        cot_block = jnp.concatenate(cot_in)
        gate_block = jnp.concatenate(gates_in)
        grad_block = (gate_block[:, None] * cot_block.astype(F32)).astype(BF)
        pre = mm("rd,hdf->hrf", row_block, weight_in)
        act, gelu_back = jax.vjp(exact_gelu, pre)
        act_low = act.astype(BF)
        expert_res = mm("hrf,hfd->rd", act_low, weight_out).astype(BF)
        grad_act = mm("rd,hfd->hrf", grad_block, weight_out)
        grad_pre = gelu_back(grad_act)[0].astype(BF)
        slot_grad = mm("hrf,hdf->rd", grad_pre, weight_in).astype(BF)
        gate_grad = jnp.sum(cot_block.astype(F32) * expert_res.astype(F32), axis=1)

        def by_sender(array):
            return list(array.reshape((experts, stride) + array.shape[1:]))

        back_grad = exchange_back(by_sender(slot_grad), "expert", experts).reshape(slots, width)
        back_gate = exchange_back(by_sender(gate_grad), "expert", experts).reshape(slots)
        back_res = exchange_back(by_sender(expert_res), "expert", experts).reshape(slots, width)

        grad_in_parts = mm("rd,hrf->hdf", row_block, grad_pre)
        grad_out_parts = mm("hrf,rd->hfd", act_low, grad_block)
        expert_sums = reduce_scatter(
            jnp.concatenate([grad_in_parts.reshape(hidden, units, width), grad_out_parts], axis=1),
            "hidden",
            hidden,
        )

        out_full = residual
        for j in range(TOPK):
            out_full = out_full + gate_values[:, j : j + 1] * mm("ts,sd->td", low_chosen[j], back_res)
        block_out = out_full.astype(BF).reshape(images.shape)

        cotangent = cot_low.astype(F32)
        grad_gate = jnp.stack(
            [jnp.sum(jnp.where(chosen[j], back_gate[None, :], 0.0), axis=1) for j in range(TOPK)],
            axis=1,
        )
        grad_routed = mm("ts,sd->td", either, back_grad)
        grad_logits = gate_back(grad_gate)[0].astype(BF)
        grad_router = mm("td,te->de", routed_low, grad_logits)
        grad_routed = grad_routed + mm("te,de->td", grad_logits, w_router)
        grad_residual, grad_second_gain, grad_second_shift = norm_two_back(grad_routed)
        grad_residual = grad_residual + cotangent
        grad_attn = grad_residual.astype(BF)
        grad_output = mm("td,te->de", mixed_heads, grad_attn)
        grad_mixed = mm("te,de->td", grad_attn, w_output).astype(BF).reshape(split_shape)
        again_probs = jnp.exp(score_block() - log_total)
        grad_probs = mm("iphd,iqhd->ihpq", grad_mixed, values)
        inner_sum = jnp.sum(grad_probs * again_probs, axis=-1, keepdims=True)
        grad_scores = (again_probs * (grad_probs - inner_sum)).astype(BF)
        grad_values = mm("ihpq,iphd->iqhd", again_probs.astype(BF), grad_mixed)
        grad_values = grad_values.astype(BF).reshape(rows, width)
        grad_queries = mm("ihpq,iqhd->iphd", grad_scores, key_rows) * scaling
        grad_queries = grad_queries.astype(BF).reshape(rows, width)
        grad_keys = mm("ihpq,iphd->iqhd", grad_scores, queries) * scaling
        grad_keys = grad_keys.astype(BF).reshape(rows, width)
        grad_query_w = mm("td,te->de", normed_low, grad_queries)
        grad_key_w = mm("td,te->de", normed_low, grad_keys)
        grad_value_w = mm("td,te->de", normed_low, grad_values)
        grad_normed = mm("te,de->td", grad_queries, w_query)
        grad_normed = grad_normed + mm("te,de->td", grad_keys, w_key)
        grad_normed = grad_normed + mm("te,de->td", grad_values, w_value)
        grad_tokens, grad_first_gain, grad_first_shift = norm_one_back(grad_normed)
        grad_images = (grad_residual + grad_tokens).reshape(images.shape)

        devices = experts * hidden

        def all_reduce(matrices):
            stacked = jnp.concatenate(matrices)
            parts = stacked.reshape(devices, -1, width)
            total = reduce_scatter(parts, world, devices).astype(BF)
            total = all_gather(total, world, devices).reshape(stacked.shape)
            return [t.astype(F32) for t in jnp.split(total, len(matrices))]

        (sum_output,) = all_reduce([grad_output])
        sum_query, sum_key, sum_value = all_reduce([grad_query_w, grad_key_w, grad_value_w])
        small_two = jnp.concatenate(
            [grad_router.T, grad_second_gain[None], grad_second_shift[None]]
        )
        small_two = all_sum(small_two, world, devices)
        small_one = all_sum(jnp.stack([grad_first_gain, grad_first_shift]), world, devices)
        return (
            block_out,
            grad_images,
            small_one[0],
            small_one[1],
            sum_query,
            sum_key,
            sum_value,
            sum_output,
            small_two[experts],
            small_two[experts + 1],
            small_two[:experts].T,
            expert_sums[:units].reshape(w_expert_in.shape),
            expert_sums[None, units:],
        )

    return on_device


def solution(mesh):
    both = ("expert", "hidden")
    return jax.shard_map(
        make_on_device(mesh.shape["expert"], mesh.shape["hidden"]),
        mesh=mesh,
        in_specs=(
            P(both, None, None),
            P(both),
            P(both, None),
            P(both, None, None),
            P(both, None, None),
            P(),
            P(),
            P(),
            P(),
            P(),
            P(),
            P(),
            P(),
            P(),
            P("expert", None, "hidden"),
            P("expert", "hidden", None),
        ),
        out_specs=(
            P(both, None, None),
            P(both, None, None),
            P(),
            P(),
            P(),
            P(),
            P(),
            P(),
            P(),
            P(),
            P(),
            P("expert", None, "hidden"),
            P("expert", "hidden", None),
        ),
        check_vma=False,
    )
```

```python
import functools

import jax
import jax.numpy as jnp
from jax import lax
from jax.experimental import pallas as pl
from jax.experimental.pallas import tpu as pltpu
from jax.sharding import PartitionSpec as P

HEADS = 8
TOPK = 2
GROUP = 4
EPSILON = 1e-06
NEGATIVE = -1e30
BF = jnp.bfloat16
F32 = jnp.float32
I32 = jnp.int32


def swap(value, axis, size, flip):
    return lax.ppermute(value, axis, [(i, i ^ flip) for i in range(size)])


def to_all(blocks, axes):
    return lax.all_to_all(blocks, axes, split_axis=0, concat_axis=0, tiled=True)


def together(*values):
    return lax.optimization_barrier(values)


def dot(left, right):
    return jnp.dot(left, right, preferred_element_type=F32)


def dot_nt(left, right):
    return lax.dot_general(left, right, (((1,), (1,)), ((), ())), preferred_element_type=F32)


def dot_tn(left, right):
    return lax.dot_general(left, right, (((0,), (0,)), ((), ())), preferred_element_type=F32)


def row_block(rows):
    return next(size for size in (336, 144, 48, 16) if rows % size == 0)


def iota(shape, dim):
    return lax.broadcasted_iota(jnp.int32, shape, dim)


def high_low(value):
    high = value.astype(BF)
    return high, (value - high.astype(F32)).astype(BF)


def normalise(values):
    average = jnp.mean(values, axis=-1, keepdims=True)
    centred = values - average
    variance = jnp.mean(centred * centred, axis=-1, keepdims=True)
    rstd = lax.rsqrt(variance + EPSILON)
    return centred * rstd, rstd


def norm_back(grad, xhat, rstd, gain):
    scaled = grad * gain
    average = jnp.mean(scaled, axis=-1, keepdims=True)
    along = jnp.mean(scaled * xhat, axis=-1, keepdims=True)
    return rstd * (scaled - average - xhat * along)


def cumulative(value):
    size = jnp.abs(value)
    base = 1.0 + 0.23164188 * size
    guess = pl.reciprocal(base, approx=True)
    t = guess * (2.0 - base * guess)
    bell = jnp.exp(-0.5 * value * value)
    poly = t * (0.127414796 + t * (-0.142248368 + t * (0.7107068705 + t * (-0.7265760135 + t * 0.5307027145))))
    tail = poly * bell
    return jnp.where(value >= 0.0, 1.0 - tail, tail), bell * 0.3989422804014327


def dispatch(targets, data, start, count):
    rows = targets.shape[1]
    slot = iota((count, rows), 0) + start
    hit = (targets[0:1, :] == slot) | (targets[1:2, :] == slot)
    return dot(jnp.where(hit, 1.0, 0.0).astype(BF), data)


def to_columns(row):
    count = row.shape[1]
    gap = -count % 128
    if gap:
        row = jnp.concatenate([row, jnp.zeros((1, gap), F32)], axis=1)
    return jnp.transpose(jnp.broadcast_to(row, (128, count + gap)))[:count]


def route_kernel(
    len_ref, pri_ref, top_ref, cot_ref, col_ref, row_ref, send_ref, column_ref, early_ref,
    *, experts, capacity, first, stride, patches,
):
    rows = pri_ref.shape[1]
    step = row_block(rows)
    token = iota((1, rows), 1)
    present = token < 0
    for i in range(rows // patches):
        present = present | ((token >= i * patches) & (token < i * patches + len_ref[i]))

    column_ref[...] = to_columns(pri_ref[...].astype(F32))
    lane = iota((step, rows), 1).astype(F32)
    place = iota((step, rows), 0).astype(F32)

    def ranks(block, total):
        base = pl.multiple_of(block * step, 16)
        hit = column_ref[pl.ds(base, step), 0:1] == lane
        here = place + (block * step).astype(F32)
        return total + jnp.sum(jnp.where(hit, here, 0.0), axis=0, keepdims=True)

    rank = lax.fori_loop(0, rows // step, ranks, jnp.zeros((1, rows), F32))
    column_ref[...] = to_columns(rank)

    def compare(block, carry):
        here = pl.ds(pl.multiple_of(block * step, 16), step)
        early_ref[here, :] = jnp.where(column_ref[here, 0:1] < rank, 1.0, 0.0).astype(BF)
        return carry

    lax.fori_loop(0, rows // step, compare, 0)
    label = iota((2 * experts, rows), 0)
    tops = [top_ref[0:1, :], top_ref[1:2, :]]
    hot = ((label == tops[0]) | (label == tops[1] + experts)) & present
    hot = jnp.where(hot, 1.0, 0.0)
    counts = dot(hot.astype(BF), early_ref[...])
    before = jnp.sum(hot[:experts], axis=1, keepdims=True)
    counts = [counts[:experts] * hot[:experts], (counts[experts:] + before) * hot[experts:]]
    found = []
    for j in range(TOPK):
        position = jnp.sum(counts[j], axis=0, keepdims=True)
        slot = (tops[j] * stride).astype(F32) + position + jnp.where(position >= first, 2.0, 0.0)
        found.append(jnp.where(present & (position < capacity), slot, -1.0))
    columns = [to_columns(f) for f in found]
    which = iota(columns[0].shape, 1)
    both = jnp.where(which == 0, columns[0], jnp.where(which == 1, columns[1], -1.0))
    col_ref[...] = both.astype(jnp.int32)
    which = iota((8, rows), 0)
    targets = jnp.where(which == 0, found[0], jnp.where(which == 1, found[1], -1.0))
    targets = targets.astype(jnp.int32)
    row_ref[...] = targets
    for e in range(experts):
        send_ref[e] = dispatch(targets, cot_ref[...], e * stride, stride).astype(BF)


def put_rows(ref, e, block, column):
    count, width = block.shape
    eye = iota((count, width), 0) == iota((count, width), 1)
    high, low = high_low(jnp.sum(jnp.where(eye, column, 0.0), axis=0, keepdims=True))
    ref[e, 0 : count - 16, :] = block[0 : count - 16].astype(BF)
    tail = iota((16, width), 0)
    last = block[count - 16 :]
    last = jnp.where(tail == 14, high.astype(F32), jnp.where(tail == 15, low.astype(F32), last))
    ref[e, count - 16 :, :] = last.astype(BF)


def get_column(ref, e):
    count, width = ref.shape[1:]
    last = jnp.where(iota((16, width), 0) >= 14, ref[e, count - 16 :, :].astype(F32), 0.0)
    eye = iota((count, width), 0) == iota((count, width), 1)
    return jnp.sum(jnp.where(eye, jnp.sum(last, axis=0, keepdims=True), 0.0), axis=1, keepdims=True)


def stack_heads(block, heads, size):
    head = iota(block.shape, 1) // size
    zero = jnp.zeros(block.shape, block.dtype)
    return jnp.concatenate([jnp.where(head == h, block, zero) for h in range(heads)])


def take_heads(stacked, heads, size):
    rows = stacked.shape[0] // heads
    head = iota((rows, stacked.shape[1]), 1) // size
    taken = stacked[:rows]
    for h in range(1, heads):
        taken = jnp.where(head == h, stacked[h * rows : (h + 1) * rows], taken)
    return taken


def forward_kernel(
    len_ref, image_ref, gain_one, shift_one, wq_ref, wk_ref, wv_ref, wo_ref, gain_two, shift_two,
    router_ref, row_ref, normed_ref, q_ref, k_ref, v_ref, prob_ref, mixed_ref, residual_ref, two_ref,
    soft_ref, send_a, send_b, side_ref, *, experts, stride, patches, group,
):
    rows, width = image_ref.shape
    size = width // HEADS
    lanes = group * size
    step = row_block(rows)

    def project(block, carry):
        here = pl.ds(pl.multiple_of(block * step, 16), step)
        xhat, _ = normalise(image_ref[here, :].astype(F32))
        normed = (xhat * gain_one[...] + shift_one[...]).astype(BF)
        normed_ref[here, :] = normed
        q_ref[here, :] = (dot(normed, wq_ref[...]) * size**-0.5).astype(BF)
        k_ref[here, :] = dot(normed, wk_ref[...]).astype(BF)
        v_ref[here, :] = dot(normed, wv_ref[...]).astype(BF)
        return carry

    lax.fori_loop(0, rows // step, project, 0)

    def attend(image, carry):
        here = pl.ds(pl.multiple_of(image * patches, 16), patches)
        length = len_ref[image]
        for g in range(HEADS // group):
            cols = pl.ds(g * lanes, lanes)
            queries = stack_heads(q_ref[here, cols], group, size)
            scores = dot_nt(k_ref[here, cols], queries)
            scores = jnp.where(iota(scores.shape, 0) < length, scores, NEGATIVE)
            top = jnp.max(scores, axis=0, keepdims=True)
            exponent = jnp.exp(scores - top)
            total = jnp.sum(exponent, axis=0, keepdims=True)
            probs = (exponent * (1.0 / total)).astype(BF)
            prob_ref[image, g] = probs
            mixed = take_heads(dot_tn(probs, v_ref[here, cols]), group, size)
            mixed_ref[here, cols] = mixed.astype(BF)
        return carry

    lax.fori_loop(0, rows // patches, attend, 0)

    def finish(block, carry):
        here = pl.ds(pl.multiple_of(block * step, 16), step)
        residual = image_ref[here, :].astype(F32) + dot(mixed_ref[here, :], wo_ref[...])
        residual_ref[here, :] = residual
        xhat, _ = normalise(residual)
        two = (xhat * gain_two[...] + shift_two[...]).astype(BF)
        two_ref[here, :] = two
        logits = dot(two, router_ref[...])
        valid = iota(logits.shape, 1) < experts
        logits = jnp.where(valid, logits, NEGATIVE)
        exponent = jnp.exp(logits - jnp.max(logits, axis=1, keepdims=True))
        soft = exponent / jnp.sum(exponent, axis=1, keepdims=True)
        soft_ref[here, :] = soft
        high, low = high_low(soft)
        side_ref[here, 0:128] = high
        side_ref[here, 128:256] = low
        return carry

    lax.fori_loop(0, rows // step, finish, 0)

    targets = row_ref[...]
    begin = 0
    for send_ref in (send_a, send_b):
        count = send_ref.shape[1]
        for e in range(experts):
            slot = iota((count, rows), 0) + (e * stride + begin)
            hit = (targets[0:1, :] == slot) | (targets[1:2, :] == slot)
            hot = jnp.where(hit, 1.0, 0.0).astype(BF)
            side = dot(hot, side_ref[...])
            side = side[:, 0:128] + side[:, 128:256]
            gate = jnp.sum(jnp.where(iota(side.shape, 1) == e, side, 0.0), axis=1, keepdims=True)
            put_rows(send_ref, e, dot(hot, two_ref[...]), gate)
        begin += count


def expert_kernel(x_ref, cot_ref, *refs, begin):
    weights, (res_ref, back_ref, act_ref, pre_ref, grad_ref) = refs[:-5], refs[-5:]
    pieces = len(weights) // 2
    chunks, count, width = x_ref.shape
    units = weights[0].shape[1]
    gates = [get_column(x_ref, c) for c in range(chunks)]
    gate = jnp.concatenate(gates)
    x = x_ref[...].reshape(chunks * count, width)
    cot = cot_ref[:, begin : begin + count, :].reshape(chunks * count, width).astype(F32)
    grad = (gate * cot).astype(BF)
    grad_ref[...] = grad.reshape(chunks, count, width)
    result = jnp.zeros((chunks * count, width), F32)
    back = jnp.zeros((chunks * count, width), F32)
    for s in range(pieces):
        cols = pl.ds(s * units, units)
        first, second = weights[s], weights[pieces + s]
        hidden = dot(x, first[...])
        below, bell = cumulative(hidden)
        act = (hidden * below).astype(BF)
        act_ref[:, :, cols] = act.reshape(chunks, count, units)
        result = result + dot(act, second[...])
        pre = (dot_nt(grad, second[...]) * (below + hidden * bell)).astype(BF)
        pre_ref[:, :, cols] = pre.reshape(chunks, count, units)
        back = back + dot_nt(pre, first[...])
    res_ref[...] = (gate * result).astype(BF).reshape(chunks, count, width)
    along = jnp.sum(cot * result, axis=1, keepdims=True)
    for c in range(chunks):
        here = slice(c * count, (c + 1) * count)
        put_rows(back_ref, c, back[here], along[here])


def expert_grad_kernel(
    x_a, x_b, pre_a, pre_b, act_a, act_b, grad_a, grad_b, in_near, in_far, out_near, out_far
):
    near = pl.program_id(0) < pl.num_programs(0) // 2
    grad_in = (dot_tn(x_a[...], pre_a[...]) + dot_tn(x_b[...], pre_b[...])).astype(BF)
    grad_out = (dot_tn(act_a[...], grad_a[...]) + dot_tn(act_b[...], grad_b[...])).astype(BF)

    @pl.when(near)
    def _():
        in_near[0] = grad_in
        out_near[0] = grad_out

    @pl.when(jnp.logical_not(near))
    def _():
        in_far[0] = grad_in
        out_far[0] = grad_out


def hot_of(col_ref, here, slots):
    columns = col_ref[here, :]
    slot = iota((columns.shape[0], slots), 1)
    hit = (columns[:, 0:1] == slot) | (columns[:, 1:2] == slot)
    return jnp.where(hit, 1.0, 0.0).astype(BF)


def backward_kernel(*refs, experts, stride, patches, group):
    (back_a, back_b, col_ref, soft_ref, residual_ref, cot_ref, two_ref, mixed_ref, normed_ref, q_ref, k_ref, v_ref, prob_ref,
     gain_two, router_ref, wo_ref,
     resid_ref, gq_ref, gk_ref, gv_ref, wg_out_ref, wg_q_ref, wg_k_ref, wg_v_ref, wg_router_ref, small_ref,
     slots_ref, attn_ref, gm_ref, logit_ref) = refs
    rows, width = cot_ref.shape
    size = width // HEADS
    lanes = group * size
    step = 144
    slots = experts * stride
    for e in range(experts):
        base = e * stride
        for back_ref in (back_a, back_b):
            here = slice(base, base + back_ref.shape[1])
            base += back_ref.shape[1]
            slots_ref[here, 0:width] = back_ref[e]
            along = get_column(back_ref, e)
            label = iota((along.shape[0], 128), 1)
            high, low = high_low(jnp.where(label == e, along, 0.0))
            slots_ref[here, width : width + 128] = high
            slots_ref[here, width + 128 : width + 256] = low

    def combine(block, carry):
        gain_sum, shift_sum = carry
        here = pl.ds(pl.multiple_of(block * step, 16), step)
        both = dot(hot_of(col_ref, here, slots), slots_ref[...])
        grad_two = both[:, 0:width]
        grad_gate = both[:, width : width + 128] + both[:, width + 128 : width + 256]
        soft = soft_ref[here, :]
        inner = jnp.sum(soft * grad_gate, axis=1, keepdims=True)
        logits = (soft * (grad_gate - inner)).astype(BF)
        logit_ref[here, :] = logits
        grad_two = grad_two + dot_nt(logits, router_ref[...])
        xhat, rstd = normalise(residual_ref[here, :])
        grad = cot_ref[here, :].astype(F32) + norm_back(grad_two, xhat, rstd, gain_two[...])
        resid_ref[here, :] = grad
        low = grad.astype(BF)
        attn_ref[here, :] = low
        gm_ref[here, :] = dot_nt(low, wo_ref[...]).astype(BF)
        gain_sum = gain_sum + jnp.sum(grad_two * xhat, axis=0, keepdims=True)
        shift_sum = shift_sum + jnp.sum(grad_two, axis=0, keepdims=True)
        return gain_sum, shift_sum

    zero = jnp.zeros((1, width), F32)
    gain_sum, shift_sum = lax.fori_loop(0, rows // step, combine, (zero, zero))
    which = iota((8, width), 0)
    small_ref[...] = jnp.where(which == 0, gain_sum, jnp.where(which == 1, shift_sum, 0.0))
    wg_router_ref[...] = dot_tn(logit_ref[...], two_ref[...])
    wg_out_ref[...] = dot_tn(mixed_ref[...], attn_ref[...]).astype(BF)

    def attend(image, carry):
        here = pl.ds(pl.multiple_of(image * patches, 16), patches)
        for g in range(HEADS // group):
            cols = pl.ds(g * lanes, lanes)
            probs = prob_ref[image, g]
            wide = probs.astype(F32)
            mixed = stack_heads(gm_ref[here, cols], group, size)
            keys = k_ref[here, cols]
            grad_probs = dot_nt(v_ref[here, cols], mixed)
            inner = jnp.sum(grad_probs * wide, axis=0, keepdims=True)
            scores = (wide * (grad_probs - inner)).astype(BF)
            gv_ref[here, cols] = dot(probs, mixed).astype(BF)
            gk_ref[here, cols] = dot(scores, stack_heads(q_ref[here, cols], group, size)).astype(BF)
            queries = take_heads(dot_tn(scores, keys), group, size)
            gq_ref[here, cols] = (queries * size**-0.5).astype(BF)
        return carry

    lax.fori_loop(0, rows // patches, attend, 0)
    wg_q_ref[...] = dot_tn(normed_ref[...], gq_ref[...]).astype(BF)
    wg_k_ref[...] = dot_tn(normed_ref[...], gk_ref[...]).astype(BF)
    wg_v_ref[...] = dot_tn(normed_ref[...], gv_ref[...]).astype(BF)


def output_kernel(col_ref, residual_ref, res_a, res_b, out_ref, slots_ref):
    step = 144
    base = 0
    for e in range(res_a.shape[0]):
        for res_ref in (res_a, res_b):
            slots_ref[base : base + res_ref.shape[1], :] = res_ref[e]
            base += res_ref.shape[1]

    def combine(block, carry):
        here = pl.ds(pl.multiple_of(block * step, 16), step)
        moe = dot(hot_of(col_ref, here, slots_ref.shape[0]), slots_ref[...])
        out_ref[here, :] = (residual_ref[here, :] + moe).astype(BF)
        return carry

    lax.fori_loop(0, residual_ref.shape[0] // step, combine, 0)


def image_kernel(gq_ref, gk_ref, gv_ref, wq_ref, wk_ref, wv_ref, image_ref, resid_ref, gain_one, out_ref, small_ref):
    rows, width = image_ref.shape
    step = row_block(rows)

    def finish(block, carry):
        gain_sum, shift_sum = carry
        here = pl.ds(pl.multiple_of(block * step, 16), step)
        grad = dot_nt(gq_ref[here, :], wq_ref[...])
        grad = grad + dot_nt(gk_ref[here, :], wk_ref[...])
        grad = grad + dot_nt(gv_ref[here, :], wv_ref[...])
        xhat, rstd = normalise(image_ref[here, :].astype(F32))
        out_ref[here, :] = resid_ref[here, :] + norm_back(grad, xhat, rstd, gain_one[...])
        gain_sum = gain_sum + jnp.sum(grad * xhat, axis=0, keepdims=True)
        shift_sum = shift_sum + jnp.sum(grad, axis=0, keepdims=True)
        return gain_sum, shift_sum

    zero = jnp.zeros((1, width), F32)
    gain_sum, shift_sum = lax.fori_loop(0, rows // step, finish, (zero, zero))
    which = iota((8, width), 0)
    small_ref[...] = jnp.where(which == 0, gain_sum, jnp.where(which == 1, shift_sum, 0.0))


COST = pl.CostEstimate(flops=0, bytes_accessed=0, transcendentals=0)
SCALAR = pl.BlockSpec(memory_space=pltpu.SMEM)
VECTOR = pl.BlockSpec(memory_space=pltpu.VMEM)


def call(kernel, outs, args, scalars=0, scratch=(), **names):
    return pl.pallas_call(
        functools.partial(kernel, **names) if names else kernel,
        out_shape=[jax.ShapeDtypeStruct(shape, kind) for shape, kind in outs],
        in_specs=[SCALAR] * scalars + [VECTOR] * (len(args) - scalars),
        out_specs=[VECTOR] * len(outs),
        scratch_shapes=scratch,
        compiler_params=pltpu.CompilerParams(vmem_limit_bytes=56 << 20),
        cost_estimate=COST,
    )(*args)


def make_on_device(experts, hidden):
    group = ("hh", "el")
    half_e, half_h = experts // 2, hidden // 2

    def over_eh(value):
        return swap(value, "eh", 2, 1)

    def moves(own):
        axes = ("eh", "hh")
        paths = ([(0, 2), (3, 1)], [(1, 0), (2, 3)], [(1, 2), (2, 1)])
        return [lax.ppermute(own, axes, pairs) for pairs in paths]

    def over_hh(value):
        return swap(value, "hh", 2, 1)

    def fold_hl(parts):
        for bit in reversed(range(half_h.bit_length() - 2)):
            count = parts.shape[0] // 2
            far = swap(parts[count:], "hl", half_h, 1 << bit)
            parts = (parts[:count].astype(F32) + far.astype(F32)).astype(BF)
        return parts

    def gather_hl(parts):
        index = lax.axis_index("hl")
        for bit in range(half_h.bit_length() - 1):
            far = swap(parts, "hl", half_h, 1 << bit)
            odd = ((index >> bit) & 1) == 1
            parts = jnp.where(odd, jnp.concatenate([far, parts]), jnp.concatenate([parts, far]))
        return parts

    def scatter_hl(parts):
        index = lax.axis_index("hl")
        for bit in reversed(range(half_h.bit_length() - 1)):
            pairs = parts.reshape((2, -1) + parts.shape[1:])
            odd = (index >> bit) & 1
            keep = lax.dynamic_index_in_dim(pairs, odd, 0, keepdims=False)
            give = lax.dynamic_index_in_dim(pairs, 1 - odd, 0, keepdims=False)
            far = swap(give, "hl", half_h, 1 << bit)
            parts = (keep.astype(F32) + far.astype(F32)).astype(BF)
        return parts[0]

    def on_device(
        images,
        lengths,
        priority,
        top_experts,
        out_grad,
        first_gain,
        first_shift,
        w_query,
        w_key,
        w_value,
        w_output,
        second_gain,
        second_shift,
        w_router,
        w_expert_in,
        w_expert_out,
    ):
        devices = experts * hidden
        image_count, patches, width = images.shape
        rows = image_count * patches
        units = w_expert_in.shape[2]
        hidden_all = units * hidden
        capacity = (21 * rows * TOPK + 20 * experts - 1) // (20 * experts)
        stride = (capacity + 4 + 15) // 16 * 16
        count_a = (stride // 2 + 15) // 16 * 16
        slots = experts * stride
        hh = lax.axis_index("hh")
        same = lax.axis_index("eh") == hh

        block = ((experts, stride, width), BF)
        block_a = ((experts, count_a, width), BF)
        block_b = ((experts, stride - count_a, width), BF)
        token_low = ((rows, width), BF)
        token_wide = ((rows, width), F32)

        own_in, own_out = w_expert_in[0], w_expert_out[0]
        moved_in, moved_out = moves(own_in), moves(own_out)

        cot = out_grad.reshape(rows, width)
        column, row, cot_send = call(
            route_kernel,
            [((rows, 128), I32), ((8, rows), I32), block],
            [lengths, priority, top_experts.reshape(rows, TOPK).T, cot],
            scalars=1,
            scratch=[pltpu.VMEM((rows, 128), F32), pltpu.VMEM((rows, rows), BF)],
            experts=experts,
            capacity=capacity,
            first=count_a - 2,
            stride=stride,
            patches=patches,
        )
        cot_in = to_all(cot_send, group)

        gain_one, shift_one, gain_two, shift_two = (
            v.reshape(1, width) for v in (first_gain, first_shift, second_gain, second_shift)
        )
        router = jnp.pad(w_router, ((0, 0), (0, 128 - experts)))
        tokens = images.reshape(rows, width)
        normed, queries, keys, values, probs, mixed, residual, two, soft, send_a, send_b = call(
            forward_kernel,
            [token_low] * 4
            + [((image_count, HEADS // GROUP, patches, GROUP * patches), BF), token_low, token_wide]
            + [token_low, ((rows, 128), F32), block_a, block_b],
            [lengths, tokens, gain_one, shift_one, w_query, w_key, w_value, w_output]
            + [gain_two, shift_two, router, row],
            scalars=1,
            scratch=[pltpu.VMEM((rows, 256), BF)],
            experts=experts,
            stride=stride,
            patches=patches,
            group=GROUP,
        )

        send_a, cot_in = together(send_a, cot_in)
        x_a = to_all(send_a, group)
        send_b, moved_in, moved_out = together(send_b, moved_in, moved_out)
        x_b = to_all(send_b, group)

        def pieces_of(own, moved):
            by_eh, by_hh, by_both = moved
            pieces = [jnp.where(same, own, by_eh), jnp.where(same, by_hh, by_both)]
            for bit in range(half_h.bit_length() - 1):
                pieces = pieces + [swap(p, "hl", half_h, 1 << bit) for p in pieces]
            return pieces

        weights = pieces_of(own_in, moved_in) + pieces_of(own_out, moved_out)

        def serve(x, begin):
            count = x.shape[1]

            def spec(rows_here, lanes):
                return pl.BlockSpec((2, rows_here, lanes), lambda i: (i, 0, 0))

            lanes_out = (width, width, hidden_all, hidden_all, width)
            return pl.pallas_call(
                functools.partial(expert_kernel, begin=begin),
                grid=(experts // 2,),
                out_shape=[jax.ShapeDtypeStruct((experts, count, n), BF) for n in lanes_out],
                in_specs=[spec(count, width), spec(stride, width)]
                + [pl.BlockSpec(w.shape, lambda i: (0, 0)) for w in weights],
                out_specs=[spec(count, n) for n in lanes_out],
                compiler_params=pltpu.CompilerParams(vmem_limit_bytes=56 << 20),
                cost_estimate=COST,
            )(x, cot_in, *weights)

        result_a, back_a, act_a, pre_a, grad_a = serve(x_a, 0)
        back_a = to_all(back_a, group)
        result_b, back_b, act_b, pre_b, grad_b = serve(x_b, count_a)
        back_b = to_all(back_b, group)

        half = hidden // 2

        def near(f):
            return (jnp.minimum(f, half - 1), 0, 0)

        def far(f):
            return (jnp.maximum(f - half, 0), 0, 0)

        def rows_of(array):
            return array.reshape(-1, array.shape[2])

        pairs = [x_a, x_b, pre_a, pre_b, act_a, act_b, grad_a, grad_b]
        pairs = [rows_of(p) for p in pairs]
        full = [pl.BlockSpec(p.shape, lambda f: (0, 0)) for p in pairs[:2]]
        part = [pl.BlockSpec((p.shape[0], units), lambda f: (0, f)) for p in pairs[:2]]
        in_near, in_far, out_near, out_far = pl.pallas_call(
            expert_grad_kernel,
            grid=(hidden,),
            out_shape=[jax.ShapeDtypeStruct((half, width, units), BF)] * 2
            + [jax.ShapeDtypeStruct((half, units, width), BF)] * 2,
            in_specs=full + part + part + full,
            out_specs=[pl.BlockSpec((1, width, units), near), pl.BlockSpec((1, width, units), far)]
            + [pl.BlockSpec((1, units, width), near), pl.BlockSpec((1, units, width), far)],
            compiler_params=pltpu.CompilerParams(vmem_limit_bytes=56 << 20),
            cost_estimate=COST,
        )(*pairs)

        def fold_far(near_parts, far_parts):
            came = swap(far_parts, "hl", half_h, half_h // 2)
            return fold_hl((near_parts.astype(F32) + came.astype(F32)).astype(BF))

        parts_in, parts_out = fold_far(in_near, in_far), fold_far(out_near, out_far)
        result_a, result_b, back_a, back_b, parts_in, parts_out = together(
            result_a, result_b, back_a, back_b, parts_in, parts_out
        )
        result_a, result_b = to_all(result_a, group), to_all(result_b, group)
        came_in, came_out = over_hh(parts_in[1]), over_hh(parts_out[1])

        resid, gq, gk, gv, wg_out, wg_q, wg_k, wg_v, wg_router, small_two = call(
            backward_kernel,
            [token_wide] + [token_low] * 3 + [((width, width), BF)] * 4
            + [((128, width), F32), ((8, width), F32)],
            [back_a, back_b, column, soft, residual, cot, two, mixed, normed, queries, keys, values, probs]
            + [gain_two, router, w_output],
            scratch=[
                pltpu.VMEM((slots, width + 256), BF),
                pltpu.VMEM((rows, width), BF),
                pltpu.VMEM((rows, width), BF),
                pltpu.VMEM((rows, 128), BF),
            ],
            experts=experts,
            stride=stride,
            patches=patches,
            group=GROUP,
        )

        wg_out, wg_q, wg_k, wg_v, gq, came_in, came_out = together(
            wg_out, wg_q, wg_k, wg_v, gq, came_in, came_out
        )

        def finish_sum(keep, came):
            return jnp.where(same, keep, came), over_eh(jnp.where(same, came, keep))

        mine_in, far_in = finish_sum(parts_in[0], came_in)
        (block_out,) = call(
            output_kernel,
            [token_low],
            [column, residual, result_a, result_b],
            scratch=[pltpu.VMEM((slots, width), BF)],
        )
        grad_images, small_one = call(
            image_kernel,
            [token_wide, ((8, width), F32)],
            [gq, gk, gv, w_query, w_key, w_value, tokens, resid, gain_one],
        )

        stacked = jnp.concatenate([wg_out, wg_q, wg_k, wg_v])
        pieces = scatter_hl(stacked.reshape(half_h, -1, width))
        pieces = to_all(pieces.reshape(experts, -1, width), group)
        pieces, far_in, came_out, block_out, small_one = together(
            pieces, far_in, came_out, block_out, small_one
        )
        mine_out, far_out = finish_sum(parts_out[0], came_out)
        piece = jnp.sum(pieces.astype(F32), axis=0)
        piece = (piece + over_eh(piece.astype(BF)).astype(F32)).astype(BF)
        pieces = to_all(jnp.broadcast_to(piece, (experts,) + piece.shape), group)
        small = jnp.concatenate([small_one[:2], small_two[:2], wg_router[:experts]])
        small = jnp.sum(to_all(jnp.broadcast_to(small, (experts,) + small.shape), group), axis=0)
        small = small + over_eh(small)
        for bit in range(half_h.bit_length() - 1):
            small = small + swap(small, "hl", half_h, 1 << bit)
        pieces, far_out, small = together(pieces, far_out, small)
        total = gather_hl(pieces.reshape(1, -1, width)).reshape(stacked.shape).astype(F32)
        sum_output, sum_query, sum_key, sum_value = jnp.split(total, 4)
        sum_in = mine_in.astype(F32) + far_in.astype(F32)
        sum_out = mine_out.astype(F32) + far_out.astype(F32)
        return (
            block_out.reshape(images.shape),
            grad_images.reshape(images.shape),
            small[0],
            small[1],
            sum_query,
            sum_key,
            sum_value,
            sum_output,
            small[2],
            small[3],
            small[4:].T,
            sum_in[None],
            sum_out[None],
        )

    return on_device


def solution(mesh):
    experts, hidden = mesh.shape["expert"], mesh.shape["hidden"]
    names = ("eh", "el", "hh", "hl")
    places = mesh.devices.reshape(2, experts // 2, 2, hidden // 2)
    tokens = (P(names, None, None), P(names), P(names, None), P(names, None, None), P(names, None, None))
    weights = (P(("eh", "el"), None, ("hh", "hl")), P(("eh", "el"), ("hh", "hl"), None))
    return jax.shard_map(
        make_on_device(experts, hidden),
        mesh=jax.sharding.Mesh(places, names),
        in_specs=tokens + (P(),) * 9 + weights,
        out_specs=(P(names, None, None),) * 2 + (P(),) * 9 + weights,
        check_vma=False,
    )
```

```python
import functools

import jax
import jax.numpy as jnp
from jax import lax
from jax.experimental import pallas as pl
from jax.experimental.pallas import tpu as pltpu
from jax.sharding import PartitionSpec as P

HEADS = 8
TOPK = 2
GROUP = 4
EPSILON = 1e-06
NEGATIVE = -1e30
BF = jnp.bfloat16
F32 = jnp.float32
I32 = jnp.int32


def swap(value, axis, size, flip):
    return lax.ppermute(value, axis, [(i, i ^ flip) for i in range(size)])


def to_all(blocks, axes):
    return lax.all_to_all(blocks, axes, split_axis=0, concat_axis=0, tiled=True)


def together(*values):
    return lax.optimization_barrier(values)


def dot(left, right):
    return jnp.dot(left, right, preferred_element_type=F32)


def dot_nt(left, right):
    return lax.dot_general(left, right, (((1,), (1,)), ((), ())), preferred_element_type=F32)


def dot_tn(left, right):
    return lax.dot_general(left, right, (((0,), (0,)), ((), ())), preferred_element_type=F32)


def row_block(rows):
    return next(size for size in (336, 144, 48, 16) if rows % size == 0)


def iota(shape, dim):
    return lax.broadcasted_iota(jnp.int32, shape, dim)


def high_low(value):
    high = value.astype(BF)
    return high, (value - high.astype(F32)).astype(BF)


def normalise(values):
    average = jnp.mean(values, axis=-1, keepdims=True)
    centred = values - average
    variance = jnp.mean(centred * centred, axis=-1, keepdims=True)
    rstd = lax.rsqrt(variance + EPSILON)
    return centred * rstd, rstd


def norm_back(grad, xhat, rstd, gain):
    scaled = grad * gain
    average = jnp.mean(scaled, axis=-1, keepdims=True)
    along = jnp.mean(scaled * xhat, axis=-1, keepdims=True)
    return rstd * (scaled - average - xhat * along)


def cumulative(value):
    t = pl.reciprocal(1.0 + 0.23164188 * jnp.abs(value), approx=True)
    bell = jnp.exp2(value * (value * -0.7213475204444817) - 1.3257480647361593)
    poly = t * (0.31938153 + t * (-0.356563782 + t * (1.781477937 + t * (-1.821255978 + t * 1.330274429))))
    tail = poly * bell
    return jnp.where(value >= 0.0, 1.0 - tail, tail), bell


def served(place, experts):
    top = experts // 2
    return place ^ ((place & (top // 2)) * 2)


def dispatch(targets, data, start, count):
    rows = targets.shape[1]
    slot = iota((count, rows), 0) + start
    hit = (targets[0:1, :] == slot) | (targets[1:2, :] == slot)
    return dot(jnp.where(hit, 1.0, 0.0).astype(BF), data)


def to_columns(row):
    count = row.shape[1]
    gap = -count % 128
    if gap:
        row = jnp.concatenate([row, jnp.zeros((1, gap), F32)], axis=1)
    return jnp.transpose(jnp.broadcast_to(row, (128, count + gap)))[:count]


def route_kernel(
    len_ref, pri_ref, top_ref, cot_ref, col_ref, row_ref, send_ref, column_ref, early_ref,
    *, experts, capacity, first, stride, patches,
):
    rows = pri_ref.shape[1]
    step = row_block(rows)
    token = iota((1, rows), 1)
    present = token < 0
    for i in range(rows // patches):
        present = present | ((token >= i * patches) & (token < i * patches + len_ref[i]))

    column_ref[...] = to_columns(pri_ref[...].astype(F32))
    lane = iota((step, rows), 1).astype(F32)
    place = iota((step, rows), 0).astype(F32)

    def ranks(block, total):
        base = pl.multiple_of(block * step, 16)
        hit = column_ref[pl.ds(base, step), 0:1] == lane
        here = place + (block * step).astype(F32)
        return total + jnp.sum(jnp.where(hit, here, 0.0), axis=0, keepdims=True)

    rank = lax.fori_loop(0, rows // step, ranks, jnp.zeros((1, rows), F32))
    column_ref[...] = to_columns(rank)

    def compare(block, carry):
        here = pl.ds(pl.multiple_of(block * step, 16), step)
        early_ref[here, :] = jnp.where(column_ref[here, 0:1] < rank, 1.0, 0.0).astype(BF)
        return carry

    lax.fori_loop(0, rows // step, compare, 0)
    label = iota((2 * experts, rows), 0)
    tops = [served(top_ref[j : j + 1, :], experts) for j in range(TOPK)]
    hot = ((label == tops[0]) | (label == tops[1] + experts)) & present
    hot = jnp.where(hot, 1.0, 0.0)
    counts = dot(hot.astype(BF), early_ref[...])
    before = jnp.sum(hot[:experts], axis=1, keepdims=True)
    counts = [counts[:experts] * hot[:experts], (counts[experts:] + before) * hot[experts:]]
    found = []
    for j in range(TOPK):
        position = jnp.sum(counts[j], axis=0, keepdims=True)
        slot = (tops[j] * stride).astype(F32) + position + jnp.where(position >= first, 2.0, 0.0)
        found.append(jnp.where(present & (position < capacity), slot, -1.0))
    columns = [to_columns(f) for f in found]
    which = iota(columns[0].shape, 1)
    both = jnp.where(which == 0, columns[0], jnp.where(which == 1, columns[1], -1.0))
    col_ref[...] = both.astype(jnp.int32)
    which = iota((8, rows), 0)
    targets = jnp.where(which == 0, found[0], jnp.where(which == 1, found[1], -1.0))
    targets = targets.astype(jnp.int32)
    row_ref[...] = targets
    for e in range(experts):
        send_ref[e] = dispatch(targets, cot_ref[...], e * stride, send_ref.shape[1]).astype(BF)


def put_rows(ref, e, block, column):
    count, width = block.shape
    eye = iota((count, width), 0) == iota((count, width), 1)
    high, low = high_low(jnp.sum(jnp.where(eye, column, 0.0), axis=0, keepdims=True))
    ref[e, 0 : count - 16, 0:width] = block[0 : count - 16].astype(BF)
    tail = iota((16, width), 0)
    last = block[count - 16 :]
    last = jnp.where(tail == 14, high.astype(F32), jnp.where(tail == 15, low.astype(F32), last))
    ref[e, count - 16 :, 0:width] = last.astype(BF)


def get_column(ref, e, width):
    count = ref.shape[1]
    last = ref[e, count - 16 :, 0:width].astype(F32)
    last = jnp.where(iota((16, width), 0) >= 14, last, 0.0)
    eye = iota((count, width), 0) == iota((count, width), 1)
    return jnp.sum(jnp.where(eye, jnp.sum(last, axis=0, keepdims=True), 0.0), axis=1, keepdims=True)


def stack_heads(block, heads, size):
    head = iota(block.shape, 1) // size
    zero = jnp.zeros(block.shape, block.dtype)
    return jnp.concatenate([jnp.where(head == h, block, zero) for h in range(heads)])


def take_heads(stacked, heads, size):
    rows = stacked.shape[0] // heads
    head = iota((rows, stacked.shape[1]), 1) // size
    taken = stacked[:rows]
    for h in range(1, heads):
        taken = jnp.where(head == h, stacked[h * rows : (h + 1) * rows], taken)
    return taken


def forward_kernel(
    len_ref, image_ref, cot_ref, gain_one, shift_one, wq_ref, wk_ref, wv_ref, wo_ref, gain_two, shift_two,
    router_ref, row_ref, normed_ref, q_ref, k_ref, v_ref, prob_ref, mixed_ref, residual_ref, two_ref,
    soft_ref, send_a, send_b, side_ref, *, experts, stride, patches, group,
):
    rows, width = image_ref.shape
    size = width // HEADS
    lanes = group * size
    step = row_block(rows)

    def project(block, carry):
        here = pl.ds(pl.multiple_of(block * step, 16), step)
        xhat, _ = normalise(image_ref[here, :].astype(F32))
        normed = (xhat * gain_one[...] + shift_one[...]).astype(BF)
        normed_ref[here, :] = normed
        q_ref[here, :] = (dot(normed, wq_ref[...]) * size**-0.5).astype(BF)
        k_ref[here, :] = dot(normed, wk_ref[...]).astype(BF)
        v_ref[here, :] = dot(normed, wv_ref[...]).astype(BF)
        return carry

    lax.fori_loop(0, rows // step, project, 0)

    def attend(image, carry):
        here = pl.ds(pl.multiple_of(image * patches, 16), patches)
        length = len_ref[image]
        for g in range(HEADS // group):
            cols = pl.ds(g * lanes, lanes)
            queries = stack_heads(q_ref[here, cols], group, size)
            scores = dot_nt(k_ref[here, cols], queries)
            scores = jnp.where(iota(scores.shape, 0) < length, scores, NEGATIVE)
            top = jnp.max(scores, axis=0, keepdims=True)
            exponent = jnp.exp(scores - top)
            total = jnp.sum(exponent, axis=0, keepdims=True)
            probs = (exponent * (1.0 / total)).astype(BF)
            prob_ref[image, g] = probs
            mixed = take_heads(dot_tn(probs, v_ref[here, cols]), group, size)
            mixed_ref[here, cols] = mixed.astype(BF)
        return carry

    lax.fori_loop(0, rows // patches, attend, 0)

    def finish(block, carry):
        here = pl.ds(pl.multiple_of(block * step, 16), step)
        residual = image_ref[here, :].astype(F32) + dot(mixed_ref[here, :], wo_ref[...])
        residual_ref[here, :] = residual
        xhat, _ = normalise(residual)
        two = (xhat * gain_two[...] + shift_two[...]).astype(BF)
        two_ref[here, :] = two
        logits = dot(two, router_ref[...])
        valid = iota(logits.shape, 1) < experts
        logits = jnp.where(valid, logits, NEGATIVE)
        exponent = jnp.exp(logits - jnp.max(logits, axis=1, keepdims=True))
        soft = exponent / jnp.sum(exponent, axis=1, keepdims=True)
        soft_ref[here, :] = soft
        high, low = high_low(soft)
        side_ref[here, 0:128] = high
        side_ref[here, 128:256] = low
        return carry

    lax.fori_loop(0, rows // step, finish, 0)

    targets = row_ref[...]
    begin = 0
    for send_ref in (send_a, send_b):
        count = send_ref.shape[1]
        for e in range(experts):
            slot = iota((count, rows), 0) + (e * stride + begin)
            hit = (targets[0:1, :] == slot) | (targets[1:2, :] == slot)
            hot = jnp.where(hit, 1.0, 0.0).astype(BF)
            side = dot(hot, side_ref[...])
            side = side[:, 0:128] + side[:, 128:256]
            gate = jnp.sum(jnp.where(iota(side.shape, 1) == served(e, experts), side, 0.0), axis=1, keepdims=True)
            put_rows(send_ref, e, dot(hot, two_ref[...]), gate)
            if begin:
                send_ref[e, :, width:] = dot(hot, cot_ref[...]).astype(BF)
        begin += count


def expert_kernel(x_ref, *refs, begin):
    first_ref, weights, outs = refs[0], refs[1:-5], refs[-5:]
    back_ref, res_ref, act_ref, pre_ref, grad_ref = outs
    chunks, count, width = back_ref.shape
    if begin:
        x_ref, cot_ref = x_ref.at[:, :, 0:width], x_ref.at[:, :, width:]
        res_ref[:, 0:begin, :] = first_ref[...]
    else:
        cot_ref = first_ref
    units = weights[0].shape[0] // 2
    gate = jnp.concatenate([get_column(x_ref, c, width) for c in range(chunks)])
    x = x_ref[...].reshape(chunks * count, width)
    cot = cot_ref[...].reshape(chunks * count, width).astype(F32)
    grad = (gate * cot).astype(BF)
    grad_ref[...] = grad.reshape(chunks, count, width)
    for s, weight in enumerate(weights):
        cols = pl.ds(s * units, units)
        hidden = dot_nt(x, weight[0:units, :])
        below, bell = cumulative(hidden)
        act_ref[:, :, cols] = (hidden * below).astype(BF).reshape(chunks, count, units)
        pre = (dot_nt(grad, weight[units:, :]) * (below + hidden * bell)).astype(BF)
        pre_ref[:, :, cols] = pre.reshape(chunks, count, units)
    act = act_ref[...].reshape(chunks * count, -1)
    pre = pre_ref[...].reshape(chunks * count, -1)
    result = dot(act, jnp.concatenate([w[units:, :] for w in weights]))
    back = dot(pre, jnp.concatenate([w[0:units, :] for w in weights]))
    res_ref[:, begin : begin + count, :] = (gate * result).astype(BF).reshape(chunks, count, width)
    along = jnp.sum(cot * result, axis=1, keepdims=True)
    for c in range(chunks):
        here = slice(c * count, (c + 1) * count)
        put_rows(back_ref, c, back[here], along[here])


def expert_grad_kernel(x_a, x_b, pre_a, pre_b, act_a, act_b, grad_a, grad_b, near_ref, far_in, far_out):
    units = pre_a.shape[1]
    near = pl.program_id(0) < pl.num_programs(0) // 2
    grad_in = (dot_tn(pre_a[...], x_a[...]) + dot_tn(pre_b[...], x_b[...])).astype(BF)
    grad_out = (dot_tn(act_a[...], grad_a[...]) + dot_tn(act_b[...], grad_b[...])).astype(BF)

    @pl.when(near)
    def _():
        near_ref[0, 0:units, :] = grad_in
        near_ref[0, units:, :] = grad_out

    @pl.when(jnp.logical_not(near))
    def _():
        far_in[0] = grad_in
        far_out[0] = grad_out


def hot_of(col_ref, here, slots):
    columns = col_ref[here, :]
    slot = iota((columns.shape[0], slots), 1)
    hit = (columns[:, 0:1] == slot) | (columns[:, 1:2] == slot)
    return jnp.where(hit, 1.0, 0.0).astype(BF)


def combine_kernel(
    back_a, back_b, col_ref, soft_ref, residual_ref, cot_ref, two_ref, mixed_ref, gain_two, router_ref, wo_ref,
    resid_ref, gm_ref, wg_out_ref, wg_router_ref, small_ref, slots_ref, attn_ref, logit_ref, *, experts, stride,
):
    rows, width = cot_ref.shape
    step = row_block(rows)
    slots = experts * stride
    for e in range(experts):
        base = e * stride
        for back_ref in (back_a, back_b):
            here = slice(base, base + back_ref.shape[1])
            base += back_ref.shape[1]
            slots_ref[here, 0:width] = back_ref[e]
            along = get_column(back_ref, e, width)
            label = iota((along.shape[0], 128), 1)
            high, low = high_low(jnp.where(label == served(e, experts), along, 0.0))
            slots_ref[here, width : width + 128] = high
            slots_ref[here, width + 128 : width + 256] = low

    def combine(block, carry):
        gain_sum, shift_sum = carry
        here = pl.ds(pl.multiple_of(block * step, 16), step)
        both = dot(hot_of(col_ref, here, slots), slots_ref[...])
        grad_two = both[:, 0:width]
        grad_gate = both[:, width : width + 128] + both[:, width + 128 : width + 256]
        soft = soft_ref[here, :]
        inner = jnp.sum(soft * grad_gate, axis=1, keepdims=True)
        logits = (soft * (grad_gate - inner)).astype(BF)
        logit_ref[here, :] = logits
        grad_two = grad_two + dot_nt(logits, router_ref[...])
        xhat, rstd = normalise(residual_ref[here, :])
        grad = cot_ref[here, :].astype(F32) + norm_back(grad_two, xhat, rstd, gain_two[...])
        resid_ref[here, :] = grad
        low = grad.astype(BF)
        attn_ref[here, :] = low
        gm_ref[here, :] = dot_nt(low, wo_ref[...]).astype(BF)
        gain_sum = gain_sum + jnp.sum(grad_two * xhat, axis=0, keepdims=True)
        shift_sum = shift_sum + jnp.sum(grad_two, axis=0, keepdims=True)
        return gain_sum, shift_sum

    zero = jnp.zeros((1, width), F32)
    gain_sum, shift_sum = lax.fori_loop(0, rows // step, combine, (zero, zero))
    which = iota((8, width), 0)
    small_ref[...] = jnp.where(which == 0, gain_sum, jnp.where(which == 1, shift_sum, 0.0))
    wg_router_ref[...] = dot_tn(logit_ref[...], two_ref[...])
    wg_out_ref[...] = dot_tn(mixed_ref[...], attn_ref[...]).astype(BF)


def attention_back_kernel(
    side_ref, gm_ref, normed_ref, q_ref, k_ref, v_ref, prob_ref, wo_ref, gq_ref, gk_ref, gv_ref, near_ref, far_one, far_two,
    *, patches, group,
):
    rows, width = gm_ref.shape
    size = width // HEADS
    lanes = group * size

    def attend(image, carry):
        here = pl.ds(pl.multiple_of(image * patches, 16), patches)
        for g in range(HEADS // group):
            cols = pl.ds(g * lanes, lanes)
            probs = prob_ref[image, g]
            wide = probs.astype(F32)
            mixed = stack_heads(gm_ref[here, cols], group, size)
            keys = k_ref[here, cols]
            grad_probs = dot_nt(v_ref[here, cols], mixed)
            inner = jnp.sum(grad_probs * wide, axis=0, keepdims=True)
            scores = (wide * (grad_probs - inner)).astype(BF)
            gv_ref[here, cols] = dot(probs, mixed).astype(BF)
            gk_ref[here, cols] = dot(scores, stack_heads(q_ref[here, cols], group, size)).astype(BF)
            queries = take_heads(dot_tn(scores, keys), group, size)
            gq_ref[here, cols] = (queries * size**-0.5).astype(BF)
        return carry

    lax.fori_loop(0, rows // patches, attend, 0)
    upper = side_ref[0] == 1
    lower = jnp.logical_not(upper)

    def put(n, value):
        @pl.when(upper if n // 2 else lower)
        def _():
            near_ref[n % 2] = value

        @pl.when(lower if n // 2 else upper)
        def _():
            (far_one, far_two)[n % 2][...] = value

    put(0, wo_ref[...])
    for n, grad_ref in enumerate((gq_ref, gk_ref, gv_ref)):
        put(n + 1, dot_tn(normed_ref[...], grad_ref[...]).astype(BF))


def output_kernel(col_ref, residual_ref, res_ref, out_ref):
    rows = residual_ref.shape[0]
    step = row_block(rows)

    def combine(block, carry):
        here = pl.ds(pl.multiple_of(block * step, 16), step)
        moe = dot(hot_of(col_ref, here, res_ref.shape[0]), res_ref[...])
        out_ref[here, :] = (residual_ref[here, :] + moe).astype(BF)
        return carry

    lax.fori_loop(0, rows // step, combine, 0)


def image_kernel(gq_ref, gk_ref, gv_ref, wq_ref, wk_ref, wv_ref, image_ref, resid_ref, gain_one, out_ref, small_ref):
    rows, width = image_ref.shape
    step = row_block(rows)

    def finish(block, carry):
        gain_sum, shift_sum = carry
        here = pl.ds(pl.multiple_of(block * step, 16), step)
        grad = dot_nt(gq_ref[here, :], wq_ref[...])
        grad = grad + dot_nt(gk_ref[here, :], wk_ref[...])
        grad = grad + dot_nt(gv_ref[here, :], wv_ref[...])
        xhat, rstd = normalise(image_ref[here, :].astype(F32))
        out_ref[here, :] = resid_ref[here, :] + norm_back(grad, xhat, rstd, gain_one[...])
        gain_sum = gain_sum + jnp.sum(grad * xhat, axis=0, keepdims=True)
        shift_sum = shift_sum + jnp.sum(grad, axis=0, keepdims=True)
        return gain_sum, shift_sum

    zero = jnp.zeros((1, width), F32)
    gain_sum, shift_sum = lax.fori_loop(0, rows // step, finish, (zero, zero))
    which = iota((8, width), 0)
    small_ref[...] = jnp.where(which == 0, gain_sum, jnp.where(which == 1, shift_sum, 0.0))


LENGTH = {
    "route": 7,
    "forward": 19,
    "expert": 21,
    "expert_grad": 16,
    "combine": 17,
    "attention_back": 1,
    "output": 1,
    "image": 1,
}


def cost(name):
    length = LENGTH[name]
    return pl.CostEstimate(flops=int(length * 1.1e9), bytes_accessed=int(length * 3.4e6), transcendentals=0)


SCALAR = pl.BlockSpec(memory_space=pltpu.SMEM)
VECTOR = pl.BlockSpec(memory_space=pltpu.VMEM)


def call(kernel, outs, args, scalars=0, scratch=(), **names):
    return pl.pallas_call(
        functools.partial(kernel, **names) if names else kernel,
        out_shape=[jax.ShapeDtypeStruct(shape, kind) for shape, kind in outs],
        in_specs=[SCALAR] * scalars + [VECTOR] * (len(args) - scalars),
        out_specs=[VECTOR] * len(outs),
        scratch_shapes=scratch,
        compiler_params=pltpu.CompilerParams(vmem_limit_bytes=56 << 20),
        cost_estimate=cost(kernel.__name__.removesuffix("_kernel")),
        name=kernel.__name__,
    )(*args)


def make_on_device(experts, hidden):
    group = ("hh", "em", "el")
    half_h = hidden // 2
    places = [(eh, em, hh) for eh in range(2) for em in range(2) for hh in range(2)]

    def step(value, home, eh, hh):
        pairs = [
            (places.index(p), places.index((p[0] ^ eh, p[1], p[2] ^ hh)))
            for p in places
            if (p[0] == p[1] ^ p[2]) == home
        ]
        return lax.ppermute(value, ("eh", "em", "hh"), pairs)

    def over_hh(value):
        return swap(value, "hh", 2, 1)

    def over_eh(value):
        return swap(value, "eh", 2, 1)

    def fold_hl(parts):
        for bit in reversed(range(half_h.bit_length() - 2)):
            count = parts.shape[0] // 2
            far = swap(parts[count:], "hl", half_h, 1 << bit)
            parts = (parts[:count].astype(F32) + far.astype(F32)).astype(BF)
        return parts

    def gather_hl(parts, count):
        index = lax.axis_index("hl")
        for bit in range(count.bit_length() - 1):
            far = swap(parts, "hl", half_h, 1 << bit)
            odd = ((index >> bit) & 1) == 1
            parts = jnp.where(odd, jnp.concatenate([far, parts]), jnp.concatenate([parts, far]))
        return parts

    def scatter_hl(parts):
        index = lax.axis_index("hl")
        for bit in reversed(range(parts.shape[0].bit_length() - 1)):
            pairs = parts.reshape((2, -1) + parts.shape[1:])
            odd = (index >> bit) & 1
            keep = lax.dynamic_index_in_dim(pairs, odd, 0, keepdims=False)
            give = lax.dynamic_index_in_dim(pairs, 1 - odd, 0, keepdims=False)
            far = swap(give, "hl", half_h, 1 << bit)
            parts = (keep.astype(F32) + far.astype(F32)).astype(BF)
        return parts[0]

    def on_device(
        images,
        lengths,
        priority,
        top_experts,
        out_grad,
        first_gain,
        first_shift,
        w_query,
        w_key,
        w_value,
        w_output,
        second_gain,
        second_shift,
        w_router,
        w_expert_in,
        w_expert_out,
    ):
        devices = experts * hidden
        image_count, patches, width = images.shape
        rows = image_count * patches
        units = w_expert_in.shape[2]
        hidden_all = units * hidden
        capacity = (21 * rows * TOPK + 20 * experts - 1) // (20 * experts)
        stride = (capacity + 4 + 15) // 16 * 16
        count_a = stride // 2 // 16 * 16
        slots = experts * stride
        hh = lax.axis_index("hh")
        home = lax.axis_index("eh") == hh ^ lax.axis_index("em")

        block_a = ((experts, count_a, width), BF)
        block_b = ((experts, stride - count_a, 2 * width), BF)
        token_low = ((rows, width), BF)
        token_wide = ((rows, width), F32)

        own = jnp.concatenate([w_expert_in[0].T, w_expert_out[0]])
        moved = [step(own, True, 1, 0), step(own, False, 0, 1), step(own, False, 1, 1)]

        cot = out_grad.reshape(rows, width)
        column, row, cot_a = call(
            route_kernel,
            [((rows, 128), I32), ((8, rows), I32), block_a],
            [lengths, priority, top_experts.reshape(rows, TOPK).T, cot],
            scalars=1,
            scratch=[pltpu.VMEM((rows, 128), F32), pltpu.VMEM((rows, rows), BF)],
            experts=experts,
            capacity=capacity,
            first=count_a - 2,
            stride=stride,
            patches=patches,
        )
        cot_a = to_all(cot_a, group)

        gain_one, shift_one, gain_two, shift_two = (
            v.reshape(1, width) for v in (first_gain, first_shift, second_gain, second_shift)
        )
        router = jnp.pad(w_router, ((0, 0), (0, 128 - experts)))
        tokens = images.reshape(rows, width)
        normed, queries, keys, values, probs, mixed, residual, two, soft, send_a, send_b = call(
            forward_kernel,
            [token_low] * 4
            + [((image_count, HEADS // GROUP, patches, GROUP * patches), BF), token_low, token_wide]
            + [token_low, ((rows, 128), F32), block_a, block_b],
            [lengths, tokens, cot, gain_one, shift_one, w_query, w_key, w_value, w_output]
            + [gain_two, shift_two, router, row],
            scalars=1,
            scratch=[pltpu.VMEM((rows, 256), BF)],
            experts=experts,
            stride=stride,
            patches=patches,
            group=GROUP,
        )

        send_a, cot_a, moved = together(send_a, cot_a, moved)
        x_a = to_all(send_a, group)
        send_b, moved = together(send_b, moved)
        x_b = to_all(send_b, group)

        by_eh, by_hh, by_both = moved
        weights = [jnp.where(home, own, by_eh), jnp.where(home, by_hh, by_both)]
        for bit in range(half_h.bit_length() - 1):
            weights = weights + [swap(w, "hl", half_h, 1 << bit) for w in weights]

        def serve(begin, *arrays):
            count = arrays[0].shape[1]

            def spec(rows_here, lanes):
                return pl.BlockSpec((2, rows_here, lanes), lambda i: (i, 0, 0))

            outs = [(count, n) for n in (width, width, hidden_all, hidden_all, width)]
            outs[1] = (begin + count, width)
            return pl.pallas_call(
                functools.partial(expert_kernel, begin=begin),
                grid=(experts // 2,),
                out_shape=[jax.ShapeDtypeStruct((experts,) + o, BF) for o in outs],
                in_specs=[spec(*a.shape[1:]) for a in arrays]
                + [pl.BlockSpec(w.shape, lambda i: (0, 0)) for w in weights],
                out_specs=[spec(*o) for o in outs],
                compiler_params=pltpu.CompilerParams(vmem_limit_bytes=56 << 20),
                cost_estimate=cost("expert"),
                name="expert_kernel",
            )(*arrays, *weights)

        back_a, result, act_a, pre_a, grad_a = serve(0, x_a, cot_a)
        back_a = to_all(back_a, group)
        back_b, result, act_b, pre_b, grad_b = serve(count_a, x_b, result)
        back_a, back_b = together(back_a, back_b)
        back_b = to_all(back_b, group)
        back_b, result = together(back_b, result)
        result = to_all(result, group)

        half = hidden // 2

        def near(f):
            return (jnp.minimum(f, half - 1), 0, 0)

        def far(f):
            return (jnp.maximum(f - half, 0), 0, 0)

        def rows_of(array):
            return array.reshape(-1, array.shape[2])

        pairs = [x_a, x_b, pre_a, pre_b, act_a, act_b, grad_a, grad_b]
        pairs = [rows_of(p) for p in pairs]
        full = [pl.BlockSpec((p.shape[0], width), lambda f: (0, 0)) for p in pairs[:2]]
        part = [pl.BlockSpec((p.shape[0], units), lambda f: (0, f)) for p in pairs[:2]]
        grads_near, *grads_far = pl.pallas_call(
            expert_grad_kernel,
            grid=(hidden,),
            out_shape=[jax.ShapeDtypeStruct((half, n, width), BF) for n in (2 * units, units, units)],
            in_specs=full + part + part + full,
            out_specs=[pl.BlockSpec((1, 2 * units, width), near)] + [pl.BlockSpec((1, units, width), far)] * 2,
            compiler_params=pltpu.CompilerParams(vmem_limit_bytes=56 << 20),
            cost_estimate=cost("expert_grad"),
            name="expert_grad_kernel",
        )(*pairs)

        came = [swap(g, "hl", half_h, half_h // 2) for g in grads_far]
        came = jnp.concatenate(came, axis=1)
        parts = fold_hl((grads_near.astype(F32) + came.astype(F32)).astype(BF))
        passed = over_hh(parts[1])
        mine, theirs = jnp.where(home, parts[0], passed), jnp.where(home, passed, parts[0])

        resid, grad_mixed, wg_out, wg_router, small_two = call(
            combine_kernel,
            [token_wide, token_low, ((width, width), BF), ((128, width), F32), ((8, width), F32)],
            [back_a, back_b, column, soft, residual, cot, two, mixed, gain_two, router, w_output],
            scratch=[
                pltpu.VMEM((slots, width + 256), BF),
                pltpu.VMEM((rows, width), BF),
                pltpu.VMEM((rows, 128), BF),
            ],
            experts=experts,
            stride=stride,
        )
        side = (lax.axis_index("hl") // (half_h // 2)).reshape(1)
        gq, gk, gv, wg_near, *wg_far = call(
            attention_back_kernel,
            [token_low] * 3 + [((2, width, width), BF)] + [((width, width), BF)] * 2,
            [side, grad_mixed, normed, queries, keys, values, probs, wg_out],
            scalars=1,
            patches=patches,
            group=GROUP,
        )

        (block_out,) = call(
            output_kernel,
            [token_low],
            [column, residual, result.reshape(slots, width)],
        )
        grad_images, small_one = call(
            image_kernel,
            [token_wide, ((8, width), F32)],
            [gq, gk, gv, w_query, w_key, w_value, tokens, resid, gain_one],
        )

        came = jnp.stack([swap(w, "hl", half_h, half_h // 2) for w in wg_far])
        pieces = (wg_near.astype(F32) + came.astype(F32)).astype(BF)
        pieces = scatter_hl(pieces.reshape(half_h // 2, -1, width))
        pieces, theirs = together(pieces, theirs)
        pieces = to_all(pieces.reshape(experts, -1, width), group)
        far_in = over_eh(theirs[:units])
        pieces, far_in, theirs, block_out, grad_images = together(pieces, far_in, theirs, block_out, grad_images)
        far_out = over_eh(theirs[units:])
        piece = jnp.sum(pieces.astype(F32), axis=0)
        piece = (piece + over_eh(piece.astype(BF)).astype(F32)).astype(BF)
        pieces = to_all(jnp.broadcast_to(piece, (experts,) + piece.shape), group)
        sum_in = (mine[:units].astype(F32) + far_in.astype(F32)).T
        sum_out = mine[units:].astype(F32) + far_out.astype(F32)
        small = jnp.concatenate([small_one[:2], small_two[:2], wg_router[:experts]])
        for axis, size in (("hl", half_h), ("el", experts // 4), ("hh", 2), ("em", 2), ("eh", 2)):
            for bit in range(size.bit_length() - 1):
                small = small + swap(small, axis, size, 1 << bit)
        pieces, small, sum_in, sum_out = together(pieces, small, sum_in, sum_out)
        pieces = gather_hl(pieces.reshape(1, -1, width), half_h // 2)
        came = swap(pieces, "hl", half_h, half_h // 2)
        lower = jnp.where(side[0] == 0, pieces, came).reshape(2, width, width).astype(F32)
        upper = jnp.where(side[0] == 0, came, pieces).reshape(2, width, width).astype(F32)
        return (
            block_out.reshape(images.shape),
            grad_images.reshape(images.shape),
            small[0],
            small[1],
            lower[1],
            upper[0],
            upper[1],
            lower[0],
            small[2],
            small[3],
            small[4:].T,
            sum_in[None],
            sum_out[None],
        )

    return on_device


def solution(mesh):
    experts, hidden = mesh.shape["expert"], mesh.shape["hidden"]
    names = ("eh", "em", "el", "hh", "hl")
    places = mesh.devices.reshape(2, 2, experts // 4, 2, hidden // 2)
    tokens = (P(names, None, None), P(names), P(names, None), P(names, None, None), P(names, None, None))
    weights = (P(names[:3], None, names[3:]), P(names[:3], names[3:], None))
    return jax.shard_map(
        make_on_device(experts, hidden),
        mesh=jax.sharding.Mesh(places, names),
        in_specs=tokens + (P(),) * 9 + weights,
        out_specs=(P(names, None, None),) * 2 + (P(),) * 9 + weights,
        check_vma=False,
    )
```

```python
import functools

import jax
import jax.numpy as jnp
from jax import lax
from jax.experimental import pallas as pl
from jax.experimental.pallas import tpu as pltpu
from jax.sharding import PartitionSpec as P

HEADS = 8
TOPK = 2
GROUP = 4
EPSILON = 1e-06
NEGATIVE = -1e30
BF = jnp.bfloat16
F32 = jnp.float32
I32 = jnp.int32


def swap(value, axis, size, flip):
    return lax.ppermute(value, axis, [(i, i ^ flip) for i in range(size)])


def to_all(blocks, axes):
    return lax.all_to_all(blocks, axes, split_axis=0, concat_axis=0, tiled=True)


def together(*values):
    return lax.optimization_barrier(values)


def dot(left, right):
    return jnp.dot(left, right, preferred_element_type=F32)


def dot_nt(left, right):
    return lax.dot_general(left, right, (((1,), (1,)), ((), ())), preferred_element_type=F32)


def dot_tn(left, right):
    return lax.dot_general(left, right, (((0,), (0,)), ((), ())), preferred_element_type=F32)


def row_block(rows):
    return next(size for size in (336, 144, 48, 16) if rows % size == 0)


def iota(shape, dim):
    return lax.broadcasted_iota(jnp.int32, shape, dim)


def high_low(value):
    high = value.astype(BF)
    return high, (value - high.astype(F32)).astype(BF)


def normalise(values):
    average = jnp.mean(values, axis=-1, keepdims=True)
    centred = values - average
    variance = jnp.mean(centred * centred, axis=-1, keepdims=True)
    rstd = lax.rsqrt(variance + EPSILON)
    return centred * rstd, rstd


def norm_back(grad, xhat, rstd, gain):
    scaled = grad * gain
    average = jnp.mean(scaled, axis=-1, keepdims=True)
    along = jnp.mean(scaled * xhat, axis=-1, keepdims=True)
    return rstd * (scaled - average - xhat * along)


def cumulative(value):
    t = pl.reciprocal(1.0 + 0.23164188 * jnp.abs(value), approx=True)
    bell = jnp.exp2(value * (value * -0.7213475204444817) - 1.3257480647361593)
    poly = t * (0.31938153 + t * (-0.356563782 + t * (1.781477937 + t * (-1.821255978 + t * 1.330274429))))
    tail = poly * bell
    return jnp.where(value >= 0.0, 1.0 - tail, tail), bell


def served(place, experts):
    top = experts // 2
    return place ^ ((place & (top // 2)) * 2)


def dispatch(targets, data, start, count):
    rows = targets.shape[1]
    slot = iota((count, rows), 0) + start
    hit = (targets[0:1, :] == slot) | (targets[1:2, :] == slot)
    return dot(jnp.where(hit, 1.0, 0.0).astype(BF), data)


def to_columns(row):
    count = row.shape[1]
    gap = -count % 128
    if gap:
        row = jnp.concatenate([row, jnp.zeros((1, gap), F32)], axis=1)
    return jnp.transpose(jnp.broadcast_to(row, (128, count + gap)))[:count]


def route_kernel(
    len_ref, pri_ref, top_ref, cot_ref, col_ref, row_ref, send_ref, column_ref, early_ref,
    *, experts, capacity, first, stride, patches,
):
    rows = pri_ref.shape[1]
    step = row_block(rows)
    token = iota((1, rows), 1)
    present = token < 0
    for i in range(rows // patches):
        present = present | ((token >= i * patches) & (token < i * patches + len_ref[i]))

    column_ref[...] = to_columns(pri_ref[...].astype(F32))
    lane = iota((step, rows), 1).astype(F32)
    place = iota((step, rows), 0).astype(F32)

    def ranks(block, total):
        base = pl.multiple_of(block * step, 16)
        hit = column_ref[pl.ds(base, step), 0:1] == lane
        here = place + (block * step).astype(F32)
        return total + jnp.sum(jnp.where(hit, here, 0.0), axis=0, keepdims=True)

    rank = lax.fori_loop(0, rows // step, ranks, jnp.zeros((1, rows), F32))
    column_ref[...] = to_columns(rank)

    def compare(block, carry):
        here = pl.ds(pl.multiple_of(block * step, 16), step)
        early_ref[here, :] = jnp.where(column_ref[here, 0:1] < rank, 1.0, 0.0).astype(BF)
        return carry

    lax.fori_loop(0, rows // step, compare, 0)
    label = iota((2 * experts, rows), 0)
    tops = [served(top_ref[j : j + 1, :], experts) for j in range(TOPK)]
    hot = ((label == tops[0]) | (label == tops[1] + experts)) & present
    hot = jnp.where(hot, 1.0, 0.0)
    counts = dot(hot.astype(BF), early_ref[...])
    before = jnp.sum(hot[:experts], axis=1, keepdims=True)
    counts = [counts[:experts] * hot[:experts], (counts[experts:] + before) * hot[experts:]]
    found = []
    for j in range(TOPK):
        position = jnp.sum(counts[j], axis=0, keepdims=True)
        slot = (tops[j] * stride).astype(F32) + position + jnp.where(position >= first, 2.0, 0.0)
        found.append(jnp.where(present & (position < capacity), slot, -1.0))
    columns = [to_columns(f) for f in found]
    which = iota(columns[0].shape, 1)
    both = jnp.where(which == 0, columns[0], jnp.where(which == 1, columns[1], -1.0))
    col_ref[...] = both.astype(jnp.int32)
    which = iota((8, rows), 0)
    targets = jnp.where(which == 0, found[0], jnp.where(which == 1, found[1], -1.0))
    targets = targets.astype(jnp.int32)
    row_ref[...] = targets
    for e in range(experts):
        send_ref[e] = dispatch(targets, cot_ref[...], e * stride, send_ref.shape[1]).astype(BF)


def put_rows(ref, e, block, column):
    count, width = block.shape
    eye = iota((count, width), 0) == iota((count, width), 1)
    high, low = high_low(jnp.sum(jnp.where(eye, column, 0.0), axis=0, keepdims=True))
    ref[e, 0 : count - 16, 0:width] = block[0 : count - 16].astype(BF)
    tail = iota((16, width), 0)
    last = block[count - 16 :]
    last = jnp.where(tail == 14, high.astype(F32), jnp.where(tail == 15, low.astype(F32), last))
    ref[e, count - 16 :, 0:width] = last.astype(BF)


def get_column(ref, e, width):
    count = ref.shape[1]
    last = ref[e, count - 16 :, 0:width].astype(F32)
    last = jnp.where(iota((16, width), 0) >= 14, last, 0.0)
    eye = iota((count, width), 0) == iota((count, width), 1)
    return jnp.sum(jnp.where(eye, jnp.sum(last, axis=0, keepdims=True), 0.0), axis=1, keepdims=True)


def stack_heads(block, heads, size):
    head = iota(block.shape, 1) // size
    zero = jnp.zeros(block.shape, block.dtype)
    return jnp.concatenate([jnp.where(head == h, block, zero) for h in range(heads)])


def take_heads(stacked, heads, size):
    rows = stacked.shape[0] // heads
    head = iota((rows, stacked.shape[1]), 1) // size
    taken = stacked[:rows]
    for h in range(1, heads):
        taken = jnp.where(head == h, stacked[h * rows : (h + 1) * rows], taken)
    return taken


def forward_kernel(
    len_ref, image_ref, cot_ref, gain_one, shift_one, wq_ref, wk_ref, wv_ref, wo_ref, gain_two, shift_two,
    router_ref, row_ref, normed_ref, q_ref, k_ref, v_ref, prob_ref, mixed_ref, residual_ref, two_ref,
    soft_ref, send_a, send_b, side_ref, *, experts, stride, patches, group,
):
    rows, width = image_ref.shape
    size = width // HEADS
    lanes = group * size
    step = row_block(rows)

    def project(block, carry):
        here = pl.ds(pl.multiple_of(block * step, 16), step)
        xhat, _ = normalise(image_ref[here, :].astype(F32))
        normed = (xhat * gain_one[...] + shift_one[...]).astype(BF)
        normed_ref[here, :] = normed
        q_ref[here, :] = (dot(normed, wq_ref[...]) * size**-0.5).astype(BF)
        k_ref[here, :] = dot(normed, wk_ref[...]).astype(BF)
        v_ref[here, :] = dot(normed, wv_ref[...]).astype(BF)
        return carry

    lax.fori_loop(0, rows // step, project, 0)

    def attend(image, carry):
        here = pl.ds(pl.multiple_of(image * patches, 16), patches)
        length = len_ref[image]
        for g in range(HEADS // group):
            cols = pl.ds(g * lanes, lanes)
            queries = stack_heads(q_ref[here, cols], group, size)
            scores = dot_nt(k_ref[here, cols], queries)
            scores = jnp.where(iota(scores.shape, 0) < length, scores, NEGATIVE)
            top = jnp.max(scores, axis=0, keepdims=True)
            exponent = jnp.exp(scores - top)
            total = jnp.sum(exponent, axis=0, keepdims=True)
            probs = (exponent * (1.0 / total)).astype(BF)
            prob_ref[image, g] = probs
            mixed = take_heads(dot_tn(probs, v_ref[here, cols]), group, size)
            mixed_ref[here, cols] = mixed.astype(BF)
        return carry

    lax.fori_loop(0, rows // patches, attend, 0)

    def finish(block, carry):
        here = pl.ds(pl.multiple_of(block * step, 16), step)
        residual = image_ref[here, :].astype(F32) + dot(mixed_ref[here, :], wo_ref[...])
        residual_ref[here, :] = residual
        xhat, _ = normalise(residual)
        two = (xhat * gain_two[...] + shift_two[...]).astype(BF)
        two_ref[here, :] = two
        logits = dot(two, router_ref[...])
        valid = iota(logits.shape, 1) < experts
        logits = jnp.where(valid, logits, NEGATIVE)
        exponent = jnp.exp(logits - jnp.max(logits, axis=1, keepdims=True))
        soft = exponent / jnp.sum(exponent, axis=1, keepdims=True)
        soft_ref[here, :] = soft
        high, low = high_low(soft)
        side_ref[here, 0:128] = high
        side_ref[here, 128:256] = low
        return carry

    lax.fori_loop(0, rows // step, finish, 0)

    targets = row_ref[...]
    begin = 0
    for send_ref in (send_a, send_b):
        count = send_ref.shape[1]
        for e in range(experts):
            slot = iota((count, rows), 0) + (e * stride + begin)
            hit = (targets[0:1, :] == slot) | (targets[1:2, :] == slot)
            hot = jnp.where(hit, 1.0, 0.0).astype(BF)
            side = dot(hot, side_ref[...])
            side = side[:, 0:128] + side[:, 128:256]
            gate = jnp.sum(jnp.where(iota(side.shape, 1) == served(e, experts), side, 0.0), axis=1, keepdims=True)
            put_rows(send_ref, e, dot(hot, two_ref[...]), gate)
            if begin:
                send_ref[e, :, width:] = dot(hot, cot_ref[...]).astype(BF)
        begin += count


def expert_kernel(x_ref, *refs, begin):
    first_ref, weights, outs = refs[0], refs[1:-5], refs[-5:]
    back_ref, res_ref, act_ref, pre_ref, grad_ref = outs
    chunks, count, width = back_ref.shape
    if begin:
        x_ref, cot_ref = x_ref.at[:, :, 0:width], x_ref.at[:, :, width:]
        res_ref[:, 0:begin, :] = first_ref[...]
    else:
        cot_ref = first_ref
    units = weights[0].shape[0] // 2
    gate = jnp.concatenate([get_column(x_ref, c, width) for c in range(chunks)])
    x = x_ref[...].reshape(chunks * count, width)
    cot = cot_ref[...].reshape(chunks * count, width).astype(F32)
    grad = (gate * cot).astype(BF)
    grad_ref[...] = grad.reshape(chunks, count, width)
    for s, weight in enumerate(weights):
        cols = pl.ds(s * units, units)
        hidden = dot_nt(x, weight[0:units, :])
        below, bell = cumulative(hidden)
        act_ref[:, :, cols] = (hidden * below).astype(BF).reshape(chunks, count, units)
        pre = (dot_nt(grad, weight[units:, :]) * (below + hidden * bell)).astype(BF)
        pre_ref[:, :, cols] = pre.reshape(chunks, count, units)
    act = act_ref[...].reshape(chunks * count, -1)
    pre = pre_ref[...].reshape(chunks * count, -1)
    result = dot(act, jnp.concatenate([w[units:, :] for w in weights]))
    back = dot(pre, jnp.concatenate([w[0:units, :] for w in weights]))
    res_ref[:, begin : begin + count, :] = (gate * result).astype(BF).reshape(chunks, count, width)
    along = jnp.sum(cot * result, axis=1, keepdims=True)
    for c in range(chunks):
        here = slice(c * count, (c + 1) * count)
        put_rows(back_ref, c, back[here], along[here])


def first_grad_kernel(x_ref, pre_ref, act_ref, grad_ref, out_ref):
    units = pre_ref.shape[1]
    out_ref[0, 0:units, :] = dot_tn(pre_ref[...], x_ref[...]).astype(BF)
    out_ref[0, units:, :] = dot_tn(act_ref[...], grad_ref[...]).astype(BF)


def second_grad_kernel(x_ref, pre_ref, act_ref, grad_ref, first_ref, near_ref, far_in, far_out):
    units = pre_ref.shape[1]
    near = pl.program_id(0) < pl.num_programs(0) // 2
    grad_in = (dot_tn(pre_ref[...], x_ref[...]) + first_ref[0, 0:units, :].astype(F32)).astype(BF)
    grad_out = (dot_tn(act_ref[...], grad_ref[...]) + first_ref[0, units:, :].astype(F32)).astype(BF)

    @pl.when(near)
    def _():
        near_ref[0, 0:units, :] = grad_in
        near_ref[0, units:, :] = grad_out

    @pl.when(jnp.logical_not(near))
    def _():
        far_in[0] = grad_in
        far_out[0] = grad_out


def hot_of(col_ref, here, slots):
    columns = col_ref[here, :]
    slot = iota((columns.shape[0], slots), 1)
    hit = (columns[:, 0:1] == slot) | (columns[:, 1:2] == slot)
    return jnp.where(hit, 1.0, 0.0).astype(BF)


def combine_kernel(
    back_a, back_b, col_ref, soft_ref, residual_ref, cot_ref, two_ref, mixed_ref, gain_two, router_ref, wo_ref,
    resid_ref, gm_ref, wg_out_ref, wg_router_ref, small_ref, slots_ref, total_ref, *, experts, stride,
):
    at = pl.program_id(0)
    width = cot_ref.shape[1]

    @pl.when(at == 0)
    def _():
        for e in range(experts):
            base = e * stride
            for back_ref in (back_a, back_b):
                here = slice(base, base + back_ref.shape[1])
                base += back_ref.shape[1]
                slots_ref[here, 0:width] = back_ref[e]
                along = get_column(back_ref, e, width)
                label = iota((along.shape[0], 128), 1)
                high, low = high_low(jnp.where(label == served(e, experts), along, 0.0))
                slots_ref[here, width : width + 128] = high
                slots_ref[here, width + 128 : width + 256] = low
        small_ref[...] = jnp.zeros(small_ref.shape, F32)
        wg_router_ref[...] = jnp.zeros(wg_router_ref.shape, F32)
        total_ref[...] = jnp.zeros(total_ref.shape, F32)

    both = dot(hot_of(col_ref, slice(None), experts * stride), slots_ref[...])
    grad_two = both[:, 0:width]
    grad_gate = both[:, width : width + 128] + both[:, width + 128 : width + 256]
    soft = soft_ref[...]
    inner = jnp.sum(soft * grad_gate, axis=1, keepdims=True)
    logits = (soft * (grad_gate - inner)).astype(BF)
    grad_two = grad_two + dot_nt(logits, router_ref[...])
    xhat, rstd = normalise(residual_ref[...])
    grad = cot_ref[...].astype(F32) + norm_back(grad_two, xhat, rstd, gain_two[...])
    resid_ref[...] = grad
    low = grad.astype(BF)
    gm_ref[...] = dot_nt(low, wo_ref[...]).astype(BF)
    which = iota(small_ref.shape, 0)
    gain_sum = jnp.sum(grad_two * xhat, axis=0, keepdims=True)
    shift_sum = jnp.sum(grad_two, axis=0, keepdims=True)
    small_ref[...] += jnp.where(which == 0, gain_sum, jnp.where(which == 1, shift_sum, 0.0))
    wg_router_ref[...] += dot_tn(logits, two_ref[...])
    total_ref[...] += dot_tn(mixed_ref[...], low)

    @pl.when(at == pl.num_programs(0) - 1)
    def _():
        wg_out_ref[...] = total_ref[...].astype(BF)


def attention_back_kernel(
    side_ref, gm_ref, q_ref, k_ref, v_ref, prob_ref, normed_ref, wo_ref, gq_ref, gk_ref, gv_ref, near_ref,
    far_0, far_1, far_2, far_3, gq_all, gk_all, gv_all, *, group,
):
    patches, width = gm_ref.shape
    size = width // HEADS
    lanes = group * size
    here = pl.ds(pl.multiple_of(pl.program_id(0) * patches, 16), patches)
    for g in range(HEADS // group):
        cols = pl.ds(g * lanes, lanes)
        probs = prob_ref[0, g]
        wide = probs.astype(F32)
        mixed = stack_heads(gm_ref[:, cols], group, size)
        grad_probs = dot_nt(v_ref[:, cols], mixed)
        inner = jnp.sum(grad_probs * wide, axis=0, keepdims=True)
        scores = (wide * (grad_probs - inner)).astype(BF)
        queries = take_heads(dot_tn(scores, k_ref[:, cols]), group, size)
        for all_ref, one_ref, value in (
            (gv_all, gv_ref, dot(probs, mixed)),
            (gk_all, gk_ref, dot(scores, stack_heads(q_ref[:, cols], group, size))),
            (gq_all, gq_ref, queries * size**-0.5),
        ):
            low = value.astype(BF)
            all_ref[here, cols] = low
            one_ref[:, cols] = low

    @pl.when(pl.program_id(0) == pl.num_programs(0) - 1)
    def _():
        upper = side_ref[0] == 1
        lower = jnp.logical_not(upper)

        def put(n, value):
            @pl.when(upper if n // 2 else lower)
            def _():
                near_ref[n % 2] = value

            @pl.when(lower if n // 2 else upper)
            def _():
                for part, ref in enumerate(((far_0, far_1), (far_2, far_3))[n % 2]):
                    ref[...] = value[part * ref.shape[0] : (part + 1) * ref.shape[0]]

        put(0, wo_ref[...])
        for n, grad_ref in enumerate((gq_all, gk_all, gv_all)):
            put(n + 1, dot_tn(normed_ref[...], grad_ref[...]).astype(BF))


def output_kernel(col_ref, residual_ref, res_ref, out_ref):
    rows = residual_ref.shape[0]
    step = row_block(rows)

    def combine(block, carry):
        here = pl.ds(pl.multiple_of(block * step, 16), step)
        moe = dot(hot_of(col_ref, here, res_ref.shape[0]), res_ref[...])
        out_ref[here, :] = (residual_ref[here, :] + moe).astype(BF)
        return carry

    lax.fori_loop(0, rows // step, combine, 0)


def image_kernel(gq_ref, gk_ref, gv_ref, wq_ref, wk_ref, wv_ref, image_ref, resid_ref, gain_one, out_ref, small_ref):
    rows, width = image_ref.shape
    step = row_block(rows)

    def finish(block, carry):
        gain_sum, shift_sum = carry
        here = pl.ds(pl.multiple_of(block * step, 16), step)
        grad = dot_nt(gq_ref[here, :], wq_ref[...])
        grad = grad + dot_nt(gk_ref[here, :], wk_ref[...])
        grad = grad + dot_nt(gv_ref[here, :], wv_ref[...])
        xhat, rstd = normalise(image_ref[here, :].astype(F32))
        out_ref[here, :] = resid_ref[here, :] + norm_back(grad, xhat, rstd, gain_one[...])
        gain_sum = gain_sum + jnp.sum(grad * xhat, axis=0, keepdims=True)
        shift_sum = shift_sum + jnp.sum(grad, axis=0, keepdims=True)
        return gain_sum, shift_sum

    zero = jnp.zeros((1, width), F32)
    gain_sum, shift_sum = lax.fori_loop(0, rows // step, finish, (zero, zero))
    which = iota((8, width), 0)
    small_ref[...] = jnp.where(which == 0, gain_sum, jnp.where(which == 1, shift_sum, 0.0))


LENGTH = {
    "route": 7,
    "forward": 19,
    "expert": 21,
    "first_grad": 9,
    "second_grad": 9,
    "combine": 17,
    "attention_back": 1,
    "output": 1,
    "image": 1,
}


def cost(name):
    length = LENGTH[name]
    return pl.CostEstimate(flops=int(length * 1.1e9), bytes_accessed=int(length * 3.4e6), transcendentals=0)


SCALAR = pl.BlockSpec(memory_space=pltpu.SMEM)
VECTOR = pl.BlockSpec(memory_space=pltpu.VMEM)


def call(kernel, outs, args, scalars=0, scratch=(), **names):
    return pl.pallas_call(
        functools.partial(kernel, **names) if names else kernel,
        out_shape=[jax.ShapeDtypeStruct(shape, kind) for shape, kind in outs],
        in_specs=[SCALAR] * scalars + [VECTOR] * (len(args) - scalars),
        out_specs=[VECTOR] * len(outs),
        scratch_shapes=scratch,
        compiler_params=pltpu.CompilerParams(vmem_limit_bytes=56 << 20),
        cost_estimate=cost(kernel.__name__.removesuffix("_kernel")),
        name=kernel.__name__,
    )(*args)


def make_on_device(experts, hidden):
    group = ("hh", "em", "el")
    half_h = hidden // 2
    places = [(eh, em, hh) for eh in range(2) for em in range(2) for hh in range(2)]

    def step(value, home, eh, hh):
        pairs = [
            (places.index(p), places.index((p[0] ^ eh, p[1], p[2] ^ hh)))
            for p in places
            if (p[0] == p[1] ^ p[2]) == home
        ]
        return lax.ppermute(value, ("eh", "em", "hh"), pairs)

    def over_hh(value):
        return swap(value, "hh", 2, 1)

    def with_three(value, axes, size):
        low, high = 1, size // 2
        one, two, three = (swap(value, axes, size, flip) for flip in (low, high, low | high))
        return (value + one) + (two + three)

    def over_eh(value):
        return swap(value, "eh", 2, 1)

    def fold_hl(parts):
        for bit in reversed(range(half_h.bit_length() - 2)):
            count = parts.shape[0] // 2
            far = swap(parts[count:], "hl", half_h, 1 << bit)
            parts = (parts[:count].astype(F32) + far.astype(F32)).astype(BF)
        return parts

    def gather_hl(parts, count):
        index = lax.axis_index("hl")
        for bit in range(count.bit_length() - 1):
            far = swap(parts, "hl", half_h, 1 << bit)
            odd = ((index >> bit) & 1) == 1
            parts = jnp.where(odd, jnp.concatenate([far, parts]), jnp.concatenate([parts, far]))
        return parts

    def scatter_hl(parts):
        index = lax.axis_index("hl")
        for bit in reversed(range(parts.shape[0].bit_length() - 1)):
            pairs = parts.reshape((2, -1) + parts.shape[1:])
            odd = (index >> bit) & 1
            keep = lax.dynamic_index_in_dim(pairs, odd, 0, keepdims=False)
            give = lax.dynamic_index_in_dim(pairs, 1 - odd, 0, keepdims=False)
            far = swap(give, "hl", half_h, 1 << bit)
            parts = (keep.astype(F32) + far.astype(F32)).astype(BF)
        return parts[0]

    def on_device(
        images,
        lengths,
        priority,
        top_experts,
        out_grad,
        first_gain,
        first_shift,
        w_query,
        w_key,
        w_value,
        w_output,
        second_gain,
        second_shift,
        w_router,
        w_expert_in,
        w_expert_out,
    ):
        devices = experts * hidden
        image_count, patches, width = images.shape
        rows = image_count * patches
        units = w_expert_in.shape[2]
        hidden_all = units * hidden
        capacity = (21 * rows * TOPK + 20 * experts - 1) // (20 * experts)
        stride = (capacity + 4 + 15) // 16 * 16
        count_a = stride // 2 // 16 * 16
        slots = experts * stride
        hh = lax.axis_index("hh")
        home = lax.axis_index("eh") == hh ^ lax.axis_index("em")

        block_a = ((experts, count_a, width), BF)
        block_b = ((experts, stride - count_a, 2 * width), BF)
        token_low = ((rows, width), BF)
        token_wide = ((rows, width), F32)

        own = jnp.concatenate([w_expert_in[0].T, w_expert_out[0]])
        moved = [step(own, True, 1, 0), step(own, False, 0, 1), step(own, False, 1, 1)]

        cot = out_grad.reshape(rows, width)
        column, row, cot_a = call(
            route_kernel,
            [((rows, 128), I32), ((8, rows), I32), block_a],
            [lengths, priority, top_experts.reshape(rows, TOPK).T, cot],
            scalars=1,
            scratch=[pltpu.VMEM((rows, 128), F32), pltpu.VMEM((rows, rows), BF)],
            experts=experts,
            capacity=capacity,
            first=count_a - 2,
            stride=stride,
            patches=patches,
        )
        cot_a = to_all(cot_a, group)

        gain_one, shift_one, gain_two, shift_two = (
            v.reshape(1, width) for v in (first_gain, first_shift, second_gain, second_shift)
        )
        router = jnp.pad(w_router, ((0, 0), (0, 128 - experts)))
        tokens = images.reshape(rows, width)
        normed, queries, keys, values, probs, mixed, residual, two, soft, send_a, send_b = call(
            forward_kernel,
            [token_low] * 4
            + [((image_count, HEADS // GROUP, patches, GROUP * patches), BF), token_low, token_wide]
            + [token_low, ((rows, 128), F32), block_a, block_b],
            [lengths, tokens, cot, gain_one, shift_one, w_query, w_key, w_value, w_output]
            + [gain_two, shift_two, router, row],
            scalars=1,
            scratch=[pltpu.VMEM((rows, 256), BF)],
            experts=experts,
            stride=stride,
            patches=patches,
            group=GROUP,
        )

        send_a, cot_a, moved = together(send_a, cot_a, moved)
        x_a = to_all(send_a, group)
        by_eh, by_hh, by_both = moved
        weights = [jnp.where(home, own, by_eh), jnp.where(home, by_hh, by_both)]
        for bit in range(half_h.bit_length() - 1):
            weights = weights + [swap(w, "hl", half_h, 1 << bit) for w in weights]
        send_b, weights = together(send_b, weights)
        x_b = to_all(send_b, group)

        def serve(begin, *arrays):
            count = arrays[0].shape[1]

            def spec(rows_here, lanes):
                return pl.BlockSpec((2, rows_here, lanes), lambda i: (i, 0, 0))

            outs = [(count, n) for n in (width, width, hidden_all, hidden_all, width)]
            outs[1] = (begin + count, width)
            return pl.pallas_call(
                functools.partial(expert_kernel, begin=begin),
                grid=(experts // 2,),
                out_shape=[jax.ShapeDtypeStruct((experts,) + o, BF) for o in outs],
                in_specs=[spec(*a.shape[1:]) for a in arrays]
                + [pl.BlockSpec(w.shape, lambda i: (0, 0)) for w in weights],
                out_specs=[spec(*o) for o in outs],
                compiler_params=pltpu.CompilerParams(vmem_limit_bytes=56 << 20),
                cost_estimate=cost("expert"),
                name="expert_kernel",
            )(*arrays, *weights)

        half = hidden // 2

        def near(f):
            return (jnp.minimum(f, half - 1), 0, 0)

        def far(f):
            return (jnp.maximum(f - half, 0), 0, 0)

        def weight_grads(kernel, x, pre, act, grad, outs, *first):
            arrays = [a.reshape(-1, a.shape[2]) for a in (x, pre, act, grad)]
            count = arrays[0].shape[0]
            full = pl.BlockSpec((count, width), lambda f: (0, 0))
            part = pl.BlockSpec((count, units), lambda f: (0, f))
            piece = [pl.BlockSpec((1,) + a.shape[1:], lambda f: (f, 0, 0)) for a in first]
            return pl.pallas_call(
                kernel,
                grid=(hidden,),
                out_shape=[jax.ShapeDtypeStruct((n, rows_here, width), BF) for n, rows_here, _ in outs],
                in_specs=[full, part, part, full] + piece,
                out_specs=[pl.BlockSpec((1, rows_here, width), at) for _, rows_here, at in outs],
                compiler_params=pltpu.CompilerParams(vmem_limit_bytes=56 << 20),
                cost_estimate=cost(kernel.__name__.removesuffix("_kernel")),
                name=kernel.__name__,
            )(*arrays, *first)

        back_a, result, act_a, pre_a, grad_a = serve(0, x_a, cot_a)
        back_a = to_all(back_a, group)
        (first,) = weight_grads(
            first_grad_kernel, x_a, pre_a, act_a, grad_a, [(hidden, 2 * units, lambda f: (f, 0, 0))]
        )
        x_b, first = together(x_b, first)
        back_b, result, act_b, pre_b, grad_b = serve(count_a, x_b, result)
        back_a, back_b = together(back_a, back_b)
        back_b = to_all(back_b, group)
        back_b, result = together(back_b, result)
        result = to_all(result, group)
        outs = [(half, 2 * units, near), (half, units, far), (half, units, far)]
        grads_near, *grads_far = weight_grads(
            second_grad_kernel, x_b, pre_b, act_b, grad_b, outs, first
        )

        came = [swap(g, "hl", half_h, half_h // 2) for g in grads_far]
        came = jnp.concatenate(came, axis=1)
        parts = fold_hl((grads_near.astype(F32) + came.astype(F32)).astype(BF))
        cut = units * 48 // 32
        passed_one, passed_two = over_hh(parts[1, :cut]), over_hh(parts[1, cut:])

        def split(keep, passed):
            return jnp.where(home, keep, passed), jnp.where(home, passed, keep)

        def blocks_of(*arrays):
            step = row_block(rows)
            return [
                pl.BlockSpec((step, a.shape[1]), lambda i: (i, 0))
                if a.shape[0] == rows
                else pl.BlockSpec(a.shape, lambda i, n=len(a.shape): (0,) * n)
                for a in arrays
            ]

        arrays = [back_a, back_b, column, soft, residual, cot, two, mixed, gain_two, router, w_output]
        outs = [token_wide, token_low, ((width, width), BF), ((128, width), F32), ((8, width), F32)]
        outs = [jax.ShapeDtypeStruct(*o) for o in outs]
        resid, grad_mixed, wg_out, wg_router, small_two = pl.pallas_call(
            functools.partial(combine_kernel, experts=experts, stride=stride),
            grid=(rows // row_block(rows),),
            out_shape=outs,
            in_specs=blocks_of(*arrays),
            out_specs=blocks_of(*outs),
            scratch_shapes=[pltpu.VMEM((slots, width + 256), BF), pltpu.VMEM((width, width), F32)],
            compiler_params=pltpu.CompilerParams(vmem_limit_bytes=56 << 20),
            cost_estimate=cost("combine"),
            name="combine_kernel",
        )(*arrays)
        side = (lax.axis_index("hl") // (half_h // 2)).reshape(1)
        one = pl.BlockSpec((patches, width), lambda i: (i, 0))
        whole = pl.BlockSpec((rows, width), lambda i: (0, 0))
        square = pl.BlockSpec((width, width), lambda i: (0, 0))
        gq, gk, gv, wg_near, *wg_far = pl.pallas_call(
            functools.partial(attention_back_kernel, group=GROUP),
            grid=(image_count,),
            out_shape=[jax.ShapeDtypeStruct((rows, width), BF)] * 3
            + [jax.ShapeDtypeStruct((2, width, width), BF)]
            + [jax.ShapeDtypeStruct((width // 2, width), BF)] * 4,
            in_specs=[SCALAR, one, one, one, one]
            + [pl.BlockSpec((1,) + probs.shape[1:], lambda i: (i, 0, 0, 0)), whole, square],
            out_specs=[one] * 3 + [pl.BlockSpec((2, width, width), lambda i: (0, 0, 0))]
            + [pl.BlockSpec((width // 2, width), lambda i: (0, 0))] * 4,
            scratch_shapes=[pltpu.VMEM((rows, width), BF)] * 3,
            compiler_params=pltpu.CompilerParams(vmem_limit_bytes=56 << 20),
            cost_estimate=cost("attention_back"),
            name="attention_back_kernel",
        )(side, grad_mixed, queries, keys, values, probs, normed, wg_out)

        (block_out,) = call(
            output_kernel,
            [token_low],
            [column, residual, result.reshape(slots, width)],
        )
        grad_images, small_one = call(
            image_kernel,
            [token_wide, ((8, width), F32)],
            [gq, gk, gv, w_query, w_key, w_value, tokens, resid, gain_one],
        )

        small = jnp.concatenate([small_one[:2], small_two[:2], wg_router[:experts]])
        others = [swap(small, ("eh", "em"), 4, flip) for flip in (1, 2, 3)]
        others, block_out = together(others, block_out)
        small = (small + others[0]) + (others[1] + others[2])

        came = jnp.concatenate([swap(w, "hl", half_h, half_h // 2) for w in wg_far]).reshape(wg_near.shape)
        pieces = (wg_near.astype(F32) + came.astype(F32)).astype(BF)
        pieces = scatter_hl(pieces.reshape(half_h // 2, -1, width))
        pieces, passed_one = together(pieces, passed_one)
        pieces = to_all(pieces.reshape(experts, -1, width), group)
        mine_one, theirs_one = split(parts[0, :cut], passed_one)
        far_one = over_eh(theirs_one)
        pieces, far_one, passed_two, block_out, grad_images, small = together(
            pieces, far_one, passed_two, block_out, grad_images, small
        )
        mine_two, theirs_two = split(parts[0, cut:], passed_two)
        far_two = over_eh(theirs_two)
        piece = jnp.sum(pieces.astype(F32), axis=0)
        piece = (piece + over_eh(piece.astype(BF)).astype(F32)).astype(BF)
        pieces = to_all(jnp.broadcast_to(piece, (experts,) + piece.shape), group)
        sums = [mine_one.astype(F32) + far_one.astype(F32), mine_two.astype(F32) + far_two.astype(F32)]
        sums = jnp.concatenate(sums)
        sum_in, sum_out = sums[:units].T, sums[units:]
        for bit in range(half_h.bit_length() - 1):
            small = small + swap(small, "hl", half_h, 1 << bit)
        for bit in range((experts // 8).bit_length() - 1):
            small = small + swap(small, "el", experts // 4, 1 << bit)
        small = with_three(small, ("el", "hh"), experts // 2)
        pieces, small, sum_in, sum_out = together(pieces, small, sum_in, sum_out)
        pieces = gather_hl(pieces.reshape(1, -1, width), half_h // 2)
        came = swap(pieces, "hl", half_h, half_h // 2)
        lower = jnp.where(side[0] == 0, pieces, came).reshape(2, width, width).astype(F32)
        upper = jnp.where(side[0] == 0, came, pieces).reshape(2, width, width).astype(F32)
        return (
            block_out.reshape(images.shape),
            grad_images.reshape(images.shape),
            small[0],
            small[1],
            lower[1],
            upper[0],
            upper[1],
            lower[0],
            small[2],
            small[3],
            small[4:].T,
            sum_in[None],
            sum_out[None],
        )

    return on_device


def solution(mesh):
    experts, hidden = mesh.shape["expert"], mesh.shape["hidden"]
    names = ("eh", "em", "el", "hh", "hl")
    places = mesh.devices.reshape(2, 2, experts // 4, 2, hidden // 2)
    tokens = (P(names, None, None), P(names), P(names, None), P(names, None, None), P(names, None, None))
    weights = (P(names[:3], None, names[3:]), P(names[:3], names[3:], None))
    return jax.shard_map(
        make_on_device(experts, hidden),
        mesh=jax.sharding.Mesh(places, names),
        in_specs=tokens + (P(),) * 9 + weights,
        out_specs=(P(names, None, None),) * 2 + (P(),) * 9 + weights,
        check_vma=False,
    )
```

```python
import functools

import jax
import jax.numpy as jnp
from jax import lax
from jax.experimental import pallas as pl
from jax.experimental.pallas import tpu as pltpu
from jax.sharding import PartitionSpec as P

HEADS = 8
TOPK = 2
GROUP = 4
EPSILON = 1e-06
NEGATIVE = -1e30
BF = jnp.bfloat16
F32 = jnp.float32
I32 = jnp.int32


def swap(value, axis, size, flip):
    return lax.ppermute(value, axis, [(i, i ^ flip) for i in range(size)])


def to_all(blocks, axes):
    return lax.all_to_all(blocks, axes, split_axis=0, concat_axis=0, tiled=True)


def together(*values):
    return lax.optimization_barrier(values)


def dot(left, right):
    return jnp.dot(left, right, preferred_element_type=F32)


def dot_nt(left, right):
    return lax.dot_general(left, right, (((1,), (1,)), ((), ())), preferred_element_type=F32)


def dot_tn(left, right):
    return lax.dot_general(left, right, (((0,), (0,)), ((), ())), preferred_element_type=F32)


def row_block(rows):
    return next(size for size in (336, 144, 48, 16) if rows % size == 0)


def iota(shape, dim):
    return lax.broadcasted_iota(jnp.int32, shape, dim)


def high_low(value):
    high = value.astype(BF)
    return high, (value - high.astype(F32)).astype(BF)


def normalise(values):
    average = jnp.mean(values, axis=-1, keepdims=True)
    centred = values - average
    variance = jnp.mean(centred * centred, axis=-1, keepdims=True)
    rstd = lax.rsqrt(variance + EPSILON)
    return centred * rstd, rstd


def norm_back(grad, xhat, rstd, gain):
    scaled = grad * gain
    average = jnp.mean(scaled, axis=-1, keepdims=True)
    along = jnp.mean(scaled * xhat, axis=-1, keepdims=True)
    return rstd * (scaled - average - xhat * along)


def cumulative(value):
    t = pl.reciprocal(1.0 + 0.23164188 * jnp.abs(value), approx=True)
    bell = jnp.exp2(value * (value * -0.7213475204444817) - 1.3257480647361593)
    poly = t * (0.31938153 + t * (-0.356563782 + t * (1.781477937 + t * (-1.821255978 + t * 1.330274429))))
    tail = poly * bell
    return jnp.where(value >= 0.0, 1.0 - tail, tail), bell


def served(place, experts):
    top = experts // 2
    return place ^ ((place & (top // 2)) * 2)


def dispatch(targets, data, start, count):
    rows = targets.shape[1]
    slot = iota((count, rows), 0) + start
    hit = (targets[0:1, :] == slot) | (targets[1:2, :] == slot)
    return dot(jnp.where(hit, 1.0, 0.0).astype(BF), data)


def to_columns(row):
    count = row.shape[1]
    gap = -count % 128
    if gap:
        row = jnp.concatenate([row, jnp.zeros((1, gap), F32)], axis=1)
    return jnp.transpose(jnp.broadcast_to(row, (128, count + gap)))[:count]


def route_kernel(
    len_ref, pri_ref, top_ref, cot_ref, col_ref, row_ref, send_ref, column_ref, early_ref,
    *, experts, capacity, first, stride, patches,
):
    rows = pri_ref.shape[1]
    step = row_block(rows)
    token = iota((1, rows), 1)
    present = token < 0
    for i in range(rows // patches):
        present = present | ((token >= i * patches) & (token < i * patches + len_ref[i]))

    column_ref[...] = to_columns(pri_ref[...].astype(F32))
    lane = iota((step, rows), 1).astype(F32)
    place = iota((step, rows), 0).astype(F32)

    def ranks(block, total):
        base = pl.multiple_of(block * step, 16)
        hit = column_ref[pl.ds(base, step), 0:1] == lane
        here = place + (block * step).astype(F32)
        return total + jnp.sum(jnp.where(hit, here, 0.0), axis=0, keepdims=True)

    rank = lax.fori_loop(0, rows // step, ranks, jnp.zeros((1, rows), F32))
    column_ref[...] = to_columns(rank)

    def compare(block, carry):
        here = pl.ds(pl.multiple_of(block * step, 16), step)
        early_ref[here, :] = jnp.where(column_ref[here, 0:1] < rank, 1.0, 0.0).astype(BF)
        return carry

    lax.fori_loop(0, rows // step, compare, 0)
    label = iota((2 * experts, rows), 0)
    tops = [served(top_ref[j : j + 1, :], experts) for j in range(TOPK)]
    hot = ((label == tops[0]) | (label == tops[1] + experts)) & present
    hot = jnp.where(hot, 1.0, 0.0)
    counts = dot(hot.astype(BF), early_ref[...])
    before = jnp.sum(hot[:experts], axis=1, keepdims=True)
    counts = [counts[:experts] * hot[:experts], (counts[experts:] + before) * hot[experts:]]
    found = []
    for j in range(TOPK):
        position = jnp.sum(counts[j], axis=0, keepdims=True)
        slot = (tops[j] * stride).astype(F32) + position + jnp.where(position >= first, 2.0, 0.0)
        found.append(jnp.where(present & (position < capacity), slot, -1.0))
    columns = [to_columns(f) for f in found]
    which = iota(columns[0].shape, 1)
    both = jnp.where(which == 0, columns[0], jnp.where(which == 1, columns[1], -1.0))
    col_ref[...] = both.astype(jnp.int32)
    which = iota((8, rows), 0)
    targets = jnp.where(which == 0, found[0], jnp.where(which == 1, found[1], -1.0))
    targets = targets.astype(jnp.int32)
    row_ref[...] = targets
    for e in range(experts):
        send_ref[e] = dispatch(targets, cot_ref[...], e * stride, send_ref.shape[1]).astype(BF)


def put_rows(ref, e, block, column):
    count, width = block.shape
    eye = iota((count, width), 0) == iota((count, width), 1)
    high, low = high_low(jnp.sum(jnp.where(eye, column, 0.0), axis=0, keepdims=True))
    ref[e, 0 : count - 16, 0:width] = block[0 : count - 16].astype(BF)
    tail = iota((16, width), 0)
    last = block[count - 16 :]
    last = jnp.where(tail == 14, high.astype(F32), jnp.where(tail == 15, low.astype(F32), last))
    ref[e, count - 16 :, 0:width] = last.astype(BF)


def get_column(ref, e, width):
    count = ref.shape[1]
    last = ref[e, count - 16 :, 0:width].astype(F32)
    last = jnp.where(iota((16, width), 0) >= 14, last, 0.0)
    eye = iota((count, width), 0) == iota((count, width), 1)
    return jnp.sum(jnp.where(eye, jnp.sum(last, axis=0, keepdims=True), 0.0), axis=1, keepdims=True)


def stack_heads(block, heads, size):
    head = iota(block.shape, 1) // size
    zero = jnp.zeros(block.shape, block.dtype)
    return jnp.concatenate([jnp.where(head == h, block, zero) for h in range(heads)])


def take_heads(stacked, heads, size):
    rows = stacked.shape[0] // heads
    head = iota((rows, stacked.shape[1]), 1) // size
    taken = stacked[:rows]
    for h in range(1, heads):
        taken = jnp.where(head == h, stacked[h * rows : (h + 1) * rows], taken)
    return taken


def forward_kernel(
    len_ref, image_ref, cot_ref, gain_one, shift_one, wq_ref, wk_ref, wv_ref, wo_ref, gain_two, shift_two,
    router_ref, row_ref, normed_ref, q_ref, k_ref, v_ref, prob_ref, mixed_ref, residual_ref, two_ref,
    soft_ref, send_a, send_b, side_ref, *, experts, stride, patches, group,
):
    rows, width = image_ref.shape
    size = width // HEADS
    lanes = group * size
    step = row_block(rows)

    def project(block, carry):
        here = pl.ds(pl.multiple_of(block * step, 16), step)
        xhat, _ = normalise(image_ref[here, :].astype(F32))
        normed = (xhat * gain_one[...] + shift_one[...]).astype(BF)
        normed_ref[here, :] = normed
        q_ref[here, :] = (dot(normed, wq_ref[...]) * size**-0.5).astype(BF)
        k_ref[here, :] = dot(normed, wk_ref[...]).astype(BF)
        v_ref[here, :] = dot(normed, wv_ref[...]).astype(BF)
        return carry

    lax.fori_loop(0, rows // step, project, 0)

    def attend(image, carry):
        here = pl.ds(pl.multiple_of(image * patches, 16), patches)
        length = len_ref[image]
        for g in range(HEADS // group):
            cols = pl.ds(g * lanes, lanes)
            queries = stack_heads(q_ref[here, cols], group, size)
            scores = dot_nt(k_ref[here, cols], queries)
            scores = jnp.where(iota(scores.shape, 0) < length, scores, NEGATIVE)
            top = jnp.max(scores, axis=0, keepdims=True)
            exponent = jnp.exp(scores - top)
            total = jnp.sum(exponent, axis=0, keepdims=True)
            probs = (exponent * (1.0 / total)).astype(BF)
            prob_ref[image, g] = probs
            mixed = take_heads(dot_tn(probs, v_ref[here, cols]), group, size)
            mixed_ref[here, cols] = mixed.astype(BF)
        return carry

    lax.fori_loop(0, rows // patches, attend, 0)

    def finish(block, carry):
        here = pl.ds(pl.multiple_of(block * step, 16), step)
        residual = image_ref[here, :].astype(F32) + dot(mixed_ref[here, :], wo_ref[...])
        residual_ref[here, :] = residual
        xhat, _ = normalise(residual)
        two = (xhat * gain_two[...] + shift_two[...]).astype(BF)
        two_ref[here, :] = two
        logits = dot(two, router_ref[...])
        valid = iota(logits.shape, 1) < experts
        logits = jnp.where(valid, logits, NEGATIVE)
        exponent = jnp.exp(logits - jnp.max(logits, axis=1, keepdims=True))
        soft = exponent / jnp.sum(exponent, axis=1, keepdims=True)
        soft_ref[here, :] = soft
        high, low = high_low(soft)
        side_ref[here, 0:128] = high
        side_ref[here, 128:256] = low
        return carry

    lax.fori_loop(0, rows // step, finish, 0)

    targets = row_ref[...]
    begin = 0
    for send_ref in (send_a, send_b):
        count = send_ref.shape[1]
        for e in range(experts):
            slot = iota((count, rows), 0) + (e * stride + begin)
            hit = (targets[0:1, :] == slot) | (targets[1:2, :] == slot)
            hot = jnp.where(hit, 1.0, 0.0).astype(BF)
            side = dot(hot, side_ref[...])
            side = side[:, 0:128] + side[:, 128:256]
            gate = jnp.sum(jnp.where(iota(side.shape, 1) == served(e, experts), side, 0.0), axis=1, keepdims=True)
            put_rows(send_ref, e, dot(hot, two_ref[...]), gate)
            if begin:
                send_ref[e, :, width:] = dot(hot, cot_ref[...]).astype(BF)
        begin += count


def expert_kernel(x_ref, *refs, begin):
    first_ref, weights, outs = refs[0], refs[1:-5], refs[-5:]
    back_ref, res_ref, act_ref, pre_ref, grad_ref = outs
    chunks, count, width = back_ref.shape
    if begin:
        x_ref, cot_ref = x_ref.at[:, :, 0:width], x_ref.at[:, :, width:]
        res_ref[:, 0:begin, :] = first_ref[...]
    else:
        cot_ref = first_ref
    units = weights[0].shape[0] // 2
    gate = jnp.concatenate([get_column(x_ref, c, width) for c in range(chunks)])
    x = x_ref[...].reshape(chunks * count, width)
    cot = cot_ref[...].reshape(chunks * count, width).astype(F32)
    grad = (gate * cot).astype(BF)
    grad_ref[...] = grad.reshape(chunks, count, width)
    for s, weight in enumerate(weights):
        cols = pl.ds(s * units, units)
        hidden = dot_nt(x, weight[0:units, :])
        below, bell = cumulative(hidden)
        act_ref[:, :, cols] = (hidden * below).astype(BF).reshape(chunks, count, units)
        pre = (dot_nt(grad, weight[units:, :]) * (below + hidden * bell)).astype(BF)
        pre_ref[:, :, cols] = pre.reshape(chunks, count, units)
    act = act_ref[...].reshape(chunks * count, -1)
    pre = pre_ref[...].reshape(chunks * count, -1)
    result = dot(act, jnp.concatenate([w[units:, :] for w in weights]))
    back = dot(pre, jnp.concatenate([w[0:units, :] for w in weights]))
    res_ref[:, begin : begin + count, :] = (gate * result).astype(BF).reshape(chunks, count, width)
    along = jnp.sum(cot * result, axis=1, keepdims=True)
    for c in range(chunks):
        here = slice(c * count, (c + 1) * count)
        put_rows(back_ref, c, back[here], along[here])


def first_grad_kernel(x_ref, pre_ref, act_ref, grad_ref, out_ref):
    units = pre_ref.shape[1]
    out_ref[0, 0:units, :] = dot_tn(pre_ref[...], x_ref[...]).astype(BF)
    out_ref[0, units:, :] = dot_tn(act_ref[...], grad_ref[...]).astype(BF)


def second_grad_kernel(x_ref, pre_ref, act_ref, grad_ref, first_ref, near_ref, far_in, far_out):
    units = pre_ref.shape[1]
    near = pl.program_id(0) < pl.num_programs(0) // 2
    grad_in = (dot_tn(pre_ref[...], x_ref[...]) + first_ref[0, 0:units, :].astype(F32)).astype(BF)
    grad_out = (dot_tn(act_ref[...], grad_ref[...]) + first_ref[0, units:, :].astype(F32)).astype(BF)

    @pl.when(near)
    def _():
        near_ref[0, 0:units, :] = grad_in
        near_ref[0, units:, :] = grad_out

    @pl.when(jnp.logical_not(near))
    def _():
        far_in[0] = grad_in
        far_out[0] = grad_out


def hot_of(col_ref, here, slots):
    columns = col_ref[here, :]
    slot = iota((columns.shape[0], slots), 1)
    hit = (columns[:, 0:1] == slot) | (columns[:, 1:2] == slot)
    return jnp.where(hit, 1.0, 0.0).astype(BF)


def combine_kernel(
    back_a, back_b, col_ref, soft_ref, residual_ref, cot_ref, two_ref, mixed_ref, gain_two, router_ref, wo_ref,
    resid_ref, gm_ref, wg_out_ref, wg_router_ref, small_ref, slots_ref, total_ref, *, experts, stride,
):
    at = pl.program_id(0)
    width = cot_ref.shape[1]

    @pl.when(at == 0)
    def _():
        for e in range(experts):
            base = e * stride
            for back_ref in (back_a, back_b):
                here = slice(base, base + back_ref.shape[1])
                base += back_ref.shape[1]
                slots_ref[here, 0:width] = back_ref[e]
                along = get_column(back_ref, e, width)
                label = iota((along.shape[0], 128), 1)
                high, low = high_low(jnp.where(label == served(e, experts), along, 0.0))
                slots_ref[here, width : width + 128] = high
                slots_ref[here, width + 128 : width + 256] = low
        small_ref[...] = jnp.zeros(small_ref.shape, F32)
        wg_router_ref[...] = jnp.zeros(wg_router_ref.shape, F32)
        total_ref[...] = jnp.zeros(total_ref.shape, F32)

    both = dot(hot_of(col_ref, slice(None), experts * stride), slots_ref[...])
    grad_two = both[:, 0:width]
    grad_gate = both[:, width : width + 128] + both[:, width + 128 : width + 256]
    soft = soft_ref[...]
    inner = jnp.sum(soft * grad_gate, axis=1, keepdims=True)
    logits = (soft * (grad_gate - inner)).astype(BF)
    grad_two = grad_two + dot_nt(logits, router_ref[...])
    xhat, rstd = normalise(residual_ref[...])
    grad = cot_ref[...].astype(F32) + norm_back(grad_two, xhat, rstd, gain_two[...])
    resid_ref[...] = grad
    low = grad.astype(BF)
    gm_ref[...] = dot_nt(low, wo_ref[...]).astype(BF)
    which = iota(small_ref.shape, 0)
    gain_sum = jnp.sum(grad_two * xhat, axis=0, keepdims=True)
    shift_sum = jnp.sum(grad_two, axis=0, keepdims=True)
    small_ref[...] += jnp.where(which == 0, gain_sum, jnp.where(which == 1, shift_sum, 0.0))
    wg_router_ref[...] += dot_tn(logits, two_ref[...])
    total_ref[...] += dot_tn(mixed_ref[...], low)

    @pl.when(at == pl.num_programs(0) - 1)
    def _():
        wg_out_ref[...] = total_ref[...].astype(BF)


def attention_back_kernel(
    side_ref, gm_ref, q_ref, k_ref, v_ref, prob_ref, normed_ref, wo_ref, gq_ref, gk_ref, gv_ref, near_ref,
    far_0, far_1, far_2, far_3, gq_all, gk_all, gv_all, *, group,
):
    patches, width = gm_ref.shape
    size = width // HEADS
    lanes = group * size
    here = pl.ds(pl.multiple_of(pl.program_id(0) * patches, 16), patches)
    for g in range(HEADS // group):
        cols = pl.ds(g * lanes, lanes)
        probs = prob_ref[0, g]
        wide = probs.astype(F32)
        mixed = stack_heads(gm_ref[:, cols], group, size)
        grad_probs = dot_nt(v_ref[:, cols], mixed)
        inner = jnp.sum(grad_probs * wide, axis=0, keepdims=True)
        scores = (wide * (grad_probs - inner)).astype(BF)
        queries = take_heads(dot_tn(scores, k_ref[:, cols]), group, size)
        for all_ref, one_ref, value in (
            (gv_all, gv_ref, dot(probs, mixed)),
            (gk_all, gk_ref, dot(scores, stack_heads(q_ref[:, cols], group, size))),
            (gq_all, gq_ref, queries * size**-0.5),
        ):
            low = value.astype(BF)
            all_ref[here, cols] = low
            one_ref[:, cols] = low

    @pl.when(pl.program_id(0) == pl.num_programs(0) - 1)
    def _():
        upper = side_ref[0] == 1
        lower = jnp.logical_not(upper)

        def put(n, value):
            @pl.when(upper if n // 2 else lower)
            def _():
                near_ref[n % 2] = value

            @pl.when(lower if n // 2 else upper)
            def _():
                for part, ref in enumerate(((far_0, far_1), (far_2, far_3))[n % 2]):
                    ref[...] = value[part * ref.shape[0] : (part + 1) * ref.shape[0]]

        put(0, wo_ref[...])
        for n, grad_ref in enumerate((gq_all, gk_all, gv_all)):
            put(n + 1, dot_tn(normed_ref[...], grad_ref[...]).astype(BF))


def output_kernel(col_ref, residual_ref, res_ref, out_ref):
    rows = residual_ref.shape[0]
    step = row_block(rows)

    def combine(block, carry):
        here = pl.ds(pl.multiple_of(block * step, 16), step)
        moe = dot(hot_of(col_ref, here, res_ref.shape[0]), res_ref[...])
        out_ref[here, :] = (residual_ref[here, :] + moe).astype(BF)
        return carry

    lax.fori_loop(0, rows // step, combine, 0)


def image_kernel(gq_ref, gk_ref, gv_ref, wq_ref, wk_ref, wv_ref, image_ref, resid_ref, gain_one, out_ref, small_ref):
    rows, width = image_ref.shape
    step = row_block(rows)

    def finish(block, carry):
        gain_sum, shift_sum = carry
        here = pl.ds(pl.multiple_of(block * step, 16), step)
        grad = dot_nt(gq_ref[here, :], wq_ref[...])
        grad = grad + dot_nt(gk_ref[here, :], wk_ref[...])
        grad = grad + dot_nt(gv_ref[here, :], wv_ref[...])
        xhat, rstd = normalise(image_ref[here, :].astype(F32))
        out_ref[here, :] = resid_ref[here, :] + norm_back(grad, xhat, rstd, gain_one[...])
        gain_sum = gain_sum + jnp.sum(grad * xhat, axis=0, keepdims=True)
        shift_sum = shift_sum + jnp.sum(grad, axis=0, keepdims=True)
        return gain_sum, shift_sum

    zero = jnp.zeros((1, width), F32)
    gain_sum, shift_sum = lax.fori_loop(0, rows // step, finish, (zero, zero))
    which = iota((8, width), 0)
    small_ref[...] = jnp.where(which == 0, gain_sum, jnp.where(which == 1, shift_sum, 0.0))


LENGTH = {
    "route": 7,
    "forward": 19,
    "expert": 21,
    "first_grad": 9,
    "second_grad": 9,
    "combine": 17,
    "attention_back": 1,
    "output": 1,
    "image": 1,
}


def cost(name):
    length = LENGTH[name]
    return pl.CostEstimate(flops=int(length * 1.1e9), bytes_accessed=int(length * 3.4e6), transcendentals=0)


SCALAR = pl.BlockSpec(memory_space=pltpu.SMEM)
VECTOR = pl.BlockSpec(memory_space=pltpu.VMEM)


def call(kernel, outs, args, scalars=0, scratch=(), **names):
    return pl.pallas_call(
        functools.partial(kernel, **names) if names else kernel,
        out_shape=[jax.ShapeDtypeStruct(shape, kind) for shape, kind in outs],
        in_specs=[SCALAR] * scalars + [VECTOR] * (len(args) - scalars),
        out_specs=[VECTOR] * len(outs),
        scratch_shapes=scratch,
        compiler_params=pltpu.CompilerParams(vmem_limit_bytes=56 << 20),
        cost_estimate=cost(kernel.__name__.removesuffix("_kernel")),
        name=kernel.__name__,
    )(*args)


def make_on_device(experts, hidden):
    group = ("hh", "em", "el")
    half_h = hidden // 2
    places = [(eh, em, hh) for eh in range(2) for em in range(2) for hh in range(2)]

    def step(value, home, eh, hh):
        pairs = [
            (places.index(p), places.index((p[0] ^ eh, p[1], p[2] ^ hh)))
            for p in places
            if (p[0] == p[1] ^ p[2]) == home
        ]
        return lax.ppermute(value, ("eh", "em", "hh"), pairs)

    def over_hh(value):
        return swap(value, "hh", 2, 1)

    def with_three(value, axes, size):
        low, high = 1, size // 2
        one, two, three = (swap(value, axes, size, flip) for flip in (low, high, low | high))
        return (value + one) + (two + three)

    def over_eh(value):
        return swap(value, "eh", 2, 1)

    def fold_hl(parts):
        for bit in reversed(range(half_h.bit_length() - 2)):
            count = parts.shape[0] // 2
            far = swap(parts[count:], "hl", half_h, 1 << bit)
            parts = (parts[:count].astype(F32) + far.astype(F32)).astype(BF)
        return parts

    def gather_hl(parts, count):
        index = lax.axis_index("hl")
        for bit in range(count.bit_length() - 1):
            far = swap(parts, "hl", half_h, 1 << bit)
            odd = ((index >> bit) & 1) == 1
            parts = jnp.where(odd, jnp.concatenate([far, parts]), jnp.concatenate([parts, far]))
        return parts

    def scatter_hl(parts):
        index = lax.axis_index("hl")
        for bit in reversed(range(parts.shape[0].bit_length() - 1)):
            pairs = parts.reshape((2, -1) + parts.shape[1:])
            odd = (index >> bit) & 1
            keep = lax.dynamic_index_in_dim(pairs, odd, 0, keepdims=False)
            give = lax.dynamic_index_in_dim(pairs, 1 - odd, 0, keepdims=False)
            far = swap(give, "hl", half_h, 1 << bit)
            parts = (keep.astype(F32) + far.astype(F32)).astype(BF)
        return parts[0]

    def on_device(
        images,
        lengths,
        priority,
        top_experts,
        out_grad,
        first_gain,
        first_shift,
        w_query,
        w_key,
        w_value,
        w_output,
        second_gain,
        second_shift,
        w_router,
        w_expert_in,
        w_expert_out,
    ):
        devices = experts * hidden
        image_count, patches, width = images.shape
        rows = image_count * patches
        units = w_expert_in.shape[2]
        hidden_all = units * hidden
        capacity = (21 * rows * TOPK + 20 * experts - 1) // (20 * experts)
        stride = (capacity + 4 + 15) // 16 * 16
        count_a = stride // 2 // 16 * 16
        slots = experts * stride
        hh = lax.axis_index("hh")
        home = lax.axis_index("eh") == hh ^ lax.axis_index("em")

        block_a = ((experts, count_a, width), BF)
        block_b = ((experts, stride - count_a, 2 * width), BF)
        token_low = ((rows, width), BF)
        token_wide = ((rows, width), F32)

        own = jnp.concatenate([w_expert_in[0].T, w_expert_out[0]])
        moved = [step(own, True, 1, 0), step(own, False, 0, 1), step(own, False, 1, 1)]

        cot = out_grad.reshape(rows, width)
        column, row, cot_a = call(
            route_kernel,
            [((rows, 128), I32), ((8, rows), I32), block_a],
            [lengths, priority, top_experts.reshape(rows, TOPK).T, cot],
            scalars=1,
            scratch=[pltpu.VMEM((rows, 128), F32), pltpu.VMEM((rows, rows), BF)],
            experts=experts,
            capacity=capacity,
            first=count_a - 2,
            stride=stride,
            patches=patches,
        )
        cot_a = to_all(cot_a, group)

        gain_one, shift_one, gain_two, shift_two = (
            v.reshape(1, width) for v in (first_gain, first_shift, second_gain, second_shift)
        )
        router = jnp.pad(w_router, ((0, 0), (0, 128 - experts)))
        tokens = images.reshape(rows, width)
        normed, queries, keys, values, probs, mixed, residual, two, soft, send_a, send_b = call(
            forward_kernel,
            [token_low] * 4
            + [((image_count, HEADS // GROUP, patches, GROUP * patches), BF), token_low, token_wide]
            + [token_low, ((rows, 128), F32), block_a, block_b],
            [lengths, tokens, cot, gain_one, shift_one, w_query, w_key, w_value, w_output]
            + [gain_two, shift_two, router, row],
            scalars=1,
            scratch=[pltpu.VMEM((rows, 256), BF)],
            experts=experts,
            stride=stride,
            patches=patches,
            group=GROUP,
        )

        send_a, cot_a, moved = together(send_a, cot_a, moved)
        x_a = to_all(send_a, group)
        by_eh, by_hh, by_both = moved
        weights = [jnp.where(home, own, by_eh), jnp.where(home, by_hh, by_both)]
        for bit in range(half_h.bit_length() - 1):
            weights = weights + [swap(w, "hl", half_h, 1 << bit) for w in weights]
        send_b, weights = together(send_b, weights)
        x_b = to_all(send_b, group)

        def serve(begin, *arrays):
            count = arrays[0].shape[1]

            def spec(rows_here, lanes):
                return pl.BlockSpec((2, rows_here, lanes), lambda i: (i, 0, 0))

            outs = [(count, n) for n in (width, width, hidden_all, hidden_all, width)]
            outs[1] = (begin + count, width)
            return pl.pallas_call(
                functools.partial(expert_kernel, begin=begin),
                grid=(experts // 2,),
                out_shape=[jax.ShapeDtypeStruct((experts,) + o, BF) for o in outs],
                in_specs=[spec(*a.shape[1:]) for a in arrays]
                + [pl.BlockSpec(w.shape, lambda i: (0, 0)) for w in weights],
                out_specs=[spec(*o) for o in outs],
                compiler_params=pltpu.CompilerParams(vmem_limit_bytes=56 << 20),
                cost_estimate=cost("expert"),
                name="expert_kernel",
            )(*arrays, *weights)

        half = hidden // 2

        def near(f):
            return (jnp.minimum(f, half - 1), 0, 0)

        def far(f):
            return (jnp.maximum(f - half, 0), 0, 0)

        def weight_grads(kernel, x, pre, act, grad, outs, *first):
            arrays = [a.reshape(-1, a.shape[2]) for a in (x, pre, act, grad)]
            count = arrays[0].shape[0]
            full = pl.BlockSpec((count, width), lambda f: (0, 0))
            part = pl.BlockSpec((count, units), lambda f: (0, f))
            piece = [pl.BlockSpec((1,) + a.shape[1:], lambda f: (f, 0, 0)) for a in first]
            return pl.pallas_call(
                kernel,
                grid=(hidden,),
                out_shape=[jax.ShapeDtypeStruct((n, rows_here, width), BF) for n, rows_here, _ in outs],
                in_specs=[full, part, part, full] + piece,
                out_specs=[pl.BlockSpec((1, rows_here, width), at) for _, rows_here, at in outs],
                compiler_params=pltpu.CompilerParams(vmem_limit_bytes=56 << 20),
                cost_estimate=cost(kernel.__name__.removesuffix("_kernel")),
                name=kernel.__name__,
            )(*arrays, *first)

        back_a, result, act_a, pre_a, grad_a = serve(0, x_a, cot_a)
        back_a = to_all(back_a, group)
        (first,) = weight_grads(
            first_grad_kernel, x_a, pre_a, act_a, grad_a, [(hidden, 2 * units, lambda f: (f, 0, 0))]
        )
        x_b, first = together(x_b, first)
        back_b, result, act_b, pre_b, grad_b = serve(count_a, x_b, result)
        back_a, back_b = together(back_a, back_b)
        back_b = to_all(back_b, group)
        back_b, result = together(back_b, result)
        result = to_all(result, group)
        outs = [(half, 2 * units, near), (half, units, far), (half, units, far)]
        grads_near, *grads_far = weight_grads(
            second_grad_kernel, x_b, pre_b, act_b, grad_b, outs, first
        )

        came = [swap(g, "hl", half_h, half_h // 2) for g in grads_far]
        came = jnp.concatenate(came, axis=1)
        parts = fold_hl((grads_near.astype(F32) + came.astype(F32)).astype(BF))
        cut = units * 44 // 32
        passed_one, passed_two = over_hh(parts[1, :cut]), over_hh(parts[1, cut:])

        def split(keep, passed):
            return jnp.where(home, keep, passed), jnp.where(home, passed, keep)

        def blocks_of(*arrays):
            step = row_block(rows)
            return [
                pl.BlockSpec((step, a.shape[1]), lambda i: (i, 0))
                if a.shape[0] == rows
                else pl.BlockSpec(a.shape, lambda i, n=len(a.shape): (0,) * n)
                for a in arrays
            ]

        arrays = [back_a, back_b, column, soft, residual, cot, two, mixed, gain_two, router, w_output]
        outs = [token_wide, token_low, ((width, width), BF), ((128, width), F32), ((8, width), F32)]
        outs = [jax.ShapeDtypeStruct(*o) for o in outs]
        resid, grad_mixed, wg_out, wg_router, small_two = pl.pallas_call(
            functools.partial(combine_kernel, experts=experts, stride=stride),
            grid=(rows // row_block(rows),),
            out_shape=outs,
            in_specs=blocks_of(*arrays),
            out_specs=blocks_of(*outs),
            scratch_shapes=[pltpu.VMEM((slots, width + 256), BF), pltpu.VMEM((width, width), F32)],
            compiler_params=pltpu.CompilerParams(vmem_limit_bytes=56 << 20),
            cost_estimate=cost("combine"),
            name="combine_kernel",
        )(*arrays)
        side = (lax.axis_index("hl") // (half_h // 2)).reshape(1)
        one = pl.BlockSpec((patches, width), lambda i: (i, 0))
        whole = pl.BlockSpec((rows, width), lambda i: (0, 0))
        square = pl.BlockSpec((width, width), lambda i: (0, 0))
        gq, gk, gv, wg_near, *wg_far = pl.pallas_call(
            functools.partial(attention_back_kernel, group=GROUP),
            grid=(image_count,),
            out_shape=[jax.ShapeDtypeStruct((rows, width), BF)] * 3
            + [jax.ShapeDtypeStruct((2, width, width), BF)]
            + [jax.ShapeDtypeStruct((width // 2, width), BF)] * 4,
            in_specs=[SCALAR, one, one, one, one]
            + [pl.BlockSpec((1,) + probs.shape[1:], lambda i: (i, 0, 0, 0)), whole, square],
            out_specs=[one] * 3 + [pl.BlockSpec((2, width, width), lambda i: (0, 0, 0))]
            + [pl.BlockSpec((width // 2, width), lambda i: (0, 0))] * 4,
            scratch_shapes=[pltpu.VMEM((rows, width), BF)] * 3,
            compiler_params=pltpu.CompilerParams(vmem_limit_bytes=56 << 20),
            cost_estimate=cost("attention_back"),
            name="attention_back_kernel",
        )(side, grad_mixed, queries, keys, values, probs, normed, wg_out)

        (block_out,) = call(
            output_kernel,
            [token_low],
            [column, residual, result.reshape(slots, width)],
        )
        grad_images, small_one = call(
            image_kernel,
            [token_wide, ((8, width), F32)],
            [gq, gk, gv, w_query, w_key, w_value, tokens, resid, gain_one],
        )

        small = jnp.concatenate([small_one[:2], small_two[:2], wg_router[:experts]])
        others = [swap(small, ("eh", "em"), 4, flip) for flip in (1, 2, 3)]
        others, block_out = together(others, block_out)
        small = (small + others[0]) + (others[1] + others[2])

        came = jnp.concatenate([swap(w, "hl", half_h, half_h // 2) for w in wg_far]).reshape(wg_near.shape)
        pieces = (wg_near.astype(F32) + came.astype(F32)).astype(BF)
        pieces = scatter_hl(pieces.reshape(half_h // 2, -1, width))
        pieces, passed_one = together(pieces, passed_one)
        pieces = to_all(pieces.reshape(experts, -1, width), group)
        mine_one, theirs_one = split(parts[0, :cut], passed_one)
        far_one = over_eh(theirs_one)
        pieces, far_one, passed_two, block_out, grad_images, small = together(
            pieces, far_one, passed_two, block_out, grad_images, small
        )
        mine_two, theirs_two = split(parts[0, cut:], passed_two)
        far_two = over_eh(theirs_two)
        piece = jnp.sum(pieces.astype(F32), axis=0)
        piece = (piece + over_eh(piece.astype(BF)).astype(F32)).astype(BF)
        pieces = to_all(jnp.broadcast_to(piece, (experts,) + piece.shape), group)
        sums = [mine_one.astype(F32) + far_one.astype(F32), mine_two.astype(F32) + far_two.astype(F32)]
        sums = jnp.concatenate(sums)
        sum_in, sum_out = sums[:units].T, sums[units:]
        for bit in range(half_h.bit_length() - 1):
            small = small + swap(small, "hl", half_h, 1 << bit)
        for bit in range((experts // 8).bit_length() - 1):
            small = small + swap(small, "el", experts // 4, 1 << bit)
        small = with_three(small, ("el", "hh"), experts // 2)
        pieces, small, sum_in, sum_out = together(pieces, small, sum_in, sum_out)
        pieces = gather_hl(pieces.reshape(1, -1, width), half_h // 2)
        came = swap(pieces, "hl", half_h, half_h // 2)
        lower = jnp.where(side[0] == 0, pieces, came).reshape(2, width, width).astype(F32)
        upper = jnp.where(side[0] == 0, came, pieces).reshape(2, width, width).astype(F32)
        return (
            block_out.reshape(images.shape),
            grad_images.reshape(images.shape),
            small[0],
            small[1],
            lower[1],
            upper[0],
            upper[1],
            lower[0],
            small[2],
            small[3],
            small[4:].T,
            sum_in[None],
            sum_out[None],
        )

    return on_device


def solution(mesh):
    experts, hidden = mesh.shape["expert"], mesh.shape["hidden"]
    names = ("eh", "em", "el", "hh", "hl")
    places = mesh.devices.reshape(2, 2, experts // 4, 2, hidden // 2)
    tokens = (P(names, None, None), P(names), P(names, None), P(names, None, None), P(names, None, None))
    weights = (P(names[:3], None, names[3:]), P(names[:3], names[3:], None))
    return jax.shard_map(
        make_on_device(experts, hidden),
        mesh=jax.sharding.Mesh(places, names),
        in_specs=tokens + (P(),) * 9 + weights,
        out_specs=(P(names, None, None),) * 2 + (P(),) * 9 + weights,
        check_vma=False,
    )
```

```python
import functools

import jax
import jax.numpy as jnp
from jax import lax
from jax.experimental import pallas as pl
from jax.experimental.pallas import tpu as pltpu
from jax.sharding import PartitionSpec as P

HEADS = 8
TOPK = 2
GROUP = 4
EPSILON = 1e-06
NEGATIVE = -1e30
BF = jnp.bfloat16
F32 = jnp.float32
I32 = jnp.int32


def swap(value, axis, size, flip):
    return lax.ppermute(value, axis, [(i, i ^ flip) for i in range(size)])


def to_all(blocks, axes):
    return lax.all_to_all(blocks, axes, split_axis=0, concat_axis=0, tiled=True)


def together(*values):
    return lax.optimization_barrier(values)


def dot(left, right):
    return jnp.dot(left, right, preferred_element_type=F32)


def dot_nt(left, right):
    return lax.dot_general(left, right, (((1,), (1,)), ((), ())), preferred_element_type=F32)


def dot_tn(left, right):
    return lax.dot_general(left, right, (((0,), (0,)), ((), ())), preferred_element_type=F32)


def row_block(rows):
    return next(size for size in (336, 144, 48, 16) if rows % size == 0)


def iota(shape, dim):
    return lax.broadcasted_iota(jnp.int32, shape, dim)


def high_low(value):
    high = value.astype(BF)
    return high, (value - high.astype(F32)).astype(BF)


def normalise(values):
    average = jnp.mean(values, axis=-1, keepdims=True)
    centred = values - average
    variance = jnp.mean(centred * centred, axis=-1, keepdims=True)
    rstd = lax.rsqrt(variance + EPSILON)
    return centred * rstd, rstd


def norm_back(grad, xhat, rstd, gain):
    scaled = grad * gain
    average = jnp.mean(scaled, axis=-1, keepdims=True)
    along = jnp.mean(scaled * xhat, axis=-1, keepdims=True)
    return rstd * (scaled - average - xhat * along)


def cumulative(value):
    t = pl.reciprocal(1.0 + 0.23164188 * jnp.abs(value), approx=True)
    bell = jnp.exp2(value * (value * -0.7213475204444817) - 1.3257480647361593)
    poly = t * (0.31938153 + t * (-0.356563782 + t * (1.781477937 + t * (-1.821255978 + t * 1.330274429))))
    tail = poly * bell
    return jnp.where(value >= 0.0, 1.0 - tail, tail), bell


def served(place, experts):
    top = experts // 2
    return place ^ ((place & (top // 2)) * 2)


def dispatch(targets, data, start, count):
    rows = targets.shape[1]
    slot = iota((count, rows), 0) + start
    hit = (targets[0:1, :] == slot) | (targets[1:2, :] == slot)
    return dot(jnp.where(hit, 1.0, 0.0).astype(BF), data)


def pack_kernel(in_ref, out_ref, both_ref):
    units = out_ref.shape[0]
    both_ref[0:units, :] = jnp.transpose(in_ref[...])
    both_ref[units:, :] = out_ref[...]


def to_columns(row):
    count = row.shape[1]
    gap = -count % 128
    if gap:
        row = jnp.concatenate([row, jnp.zeros((1, gap), F32)], axis=1)
    return jnp.transpose(jnp.broadcast_to(row, (128, count + gap)))[:count]


def route_kernel(
    len_ref, pri_ref, top_ref, cot_ref, col_ref, row_ref, send_ref, column_ref, early_ref,
    *, experts, capacity, first, stride, patches,
):
    rows = pri_ref.shape[1]
    step = row_block(rows)
    token = iota((1, rows), 1)
    present = token < 0
    for i in range(rows // patches):
        present = present | ((token >= i * patches) & (token < i * patches + len_ref[i]))

    column_ref[...] = to_columns(pri_ref[...].astype(F32))
    lane = iota((step, rows), 1).astype(F32)
    place = iota((step, rows), 0).astype(F32)

    def ranks(block, total):
        base = pl.multiple_of(block * step, 16)
        hit = column_ref[pl.ds(base, step), 0:1] == lane
        here = place + (block * step).astype(F32)
        return total + jnp.sum(jnp.where(hit, here, 0.0), axis=0, keepdims=True)

    rank = lax.fori_loop(0, rows // step, ranks, jnp.zeros((1, rows), F32))
    column_ref[...] = to_columns(rank)

    def compare(block, carry):
        here = pl.ds(pl.multiple_of(block * step, 16), step)
        early_ref[here, :] = jnp.where(column_ref[here, 0:1] < rank, 1.0, 0.0).astype(BF)
        return carry

    lax.fori_loop(0, rows // step, compare, 0)
    label = iota((2 * experts, rows), 0)
    tops = [served(top_ref[j : j + 1, :], experts) for j in range(TOPK)]
    hot = ((label == tops[0]) | (label == tops[1] + experts)) & present
    hot = jnp.where(hot, 1.0, 0.0)
    counts = dot(hot.astype(BF), early_ref[...])
    before = jnp.sum(hot[:experts], axis=1, keepdims=True)
    counts = [counts[:experts] * hot[:experts], (counts[experts:] + before) * hot[experts:]]
    found = []
    for j in range(TOPK):
        position = jnp.sum(counts[j], axis=0, keepdims=True)
        slot = (tops[j] * stride).astype(F32) + position + jnp.where(position >= first, 2.0, 0.0)
        found.append(jnp.where(present & (position < capacity), slot, -1.0))
    columns = [to_columns(f) for f in found]
    which = iota(columns[0].shape, 1)
    both = jnp.where(which == 0, columns[0], jnp.where(which == 1, columns[1], -1.0))
    col_ref[...] = both.astype(jnp.int32)
    which = iota((8, rows), 0)
    targets = jnp.where(which == 0, found[0], jnp.where(which == 1, found[1], -1.0))
    targets = targets.astype(jnp.int32)
    row_ref[...] = targets
    for e in range(experts):
        send_ref[e] = dispatch(targets, cot_ref[...], e * stride, send_ref.shape[1]).astype(BF)


def put_rows(ref, e, block, column):
    count, width = block.shape
    eye = iota((count, width), 0) == iota((count, width), 1)
    high, low = high_low(jnp.sum(jnp.where(eye, column, 0.0), axis=0, keepdims=True))
    ref[e, 0 : count - 16, 0:width] = block[0 : count - 16].astype(BF)
    tail = iota((16, width), 0)
    last = block[count - 16 :]
    last = jnp.where(tail == 14, high.astype(F32), jnp.where(tail == 15, low.astype(F32), last))
    ref[e, count - 16 :, 0:width] = last.astype(BF)


def get_column(ref, e, width):
    count = ref.shape[1]
    last = ref[e, count - 16 :, 0:width].astype(F32)
    last = jnp.where(iota((16, width), 0) >= 14, last, 0.0)
    eye = iota((count, width), 0) == iota((count, width), 1)
    return jnp.sum(jnp.where(eye, jnp.sum(last, axis=0, keepdims=True), 0.0), axis=1, keepdims=True)


def stack_heads(block, heads, size):
    head = iota(block.shape, 1) // size
    zero = jnp.zeros(block.shape, block.dtype)
    return jnp.concatenate([jnp.where(head == h, block, zero) for h in range(heads)])


def take_heads(stacked, heads, size):
    rows = stacked.shape[0] // heads
    head = iota((rows, stacked.shape[1]), 1) // size
    taken = stacked[:rows]
    for h in range(1, heads):
        taken = jnp.where(head == h, stacked[h * rows : (h + 1) * rows], taken)
    return taken


def forward_kernel(
    len_ref, image_ref, cot_ref, gain_one, shift_one, wq_ref, wk_ref, wv_ref, wo_ref, gain_two, shift_two,
    router_ref, row_ref, normed_ref, q_ref, k_ref, v_ref, prob_ref, mixed_ref, residual_ref, two_ref,
    soft_ref, send_a, send_b, side_ref, *, experts, stride, patches, group,
):
    rows, width = image_ref.shape
    size = width // HEADS
    lanes = group * size
    step = row_block(rows)

    def project(block, carry):
        here = pl.ds(pl.multiple_of(block * step, 16), step)
        xhat, _ = normalise(image_ref[here, :].astype(F32))
        normed = (xhat * gain_one[...] + shift_one[...]).astype(BF)
        normed_ref[here, :] = normed
        q_ref[here, :] = (dot(normed, wq_ref[...]) * size**-0.5).astype(BF)
        k_ref[here, :] = dot(normed, wk_ref[...]).astype(BF)
        v_ref[here, :] = dot(normed, wv_ref[...]).astype(BF)
        return carry

    lax.fori_loop(0, rows // step, project, 0)

    def attend(image, carry):
        here = pl.ds(pl.multiple_of(image * patches, 16), patches)
        length = len_ref[image]
        for g in range(HEADS // group):
            cols = pl.ds(g * lanes, lanes)
            queries = stack_heads(q_ref[here, cols], group, size)
            scores = dot_nt(k_ref[here, cols], queries)
            scores = jnp.where(iota(scores.shape, 0) < length, scores, NEGATIVE)
            top = jnp.max(scores, axis=0, keepdims=True)
            exponent = jnp.exp(scores - top)
            total = jnp.sum(exponent, axis=0, keepdims=True)
            probs = (exponent * (1.0 / total)).astype(BF)
            prob_ref[image, g] = probs
            mixed = take_heads(dot_tn(probs, v_ref[here, cols]), group, size)
            mixed_ref[here, cols] = mixed.astype(BF)
        return carry

    lax.fori_loop(0, rows // patches, attend, 0)

    def finish(block, carry):
        here = pl.ds(pl.multiple_of(block * step, 16), step)
        residual = image_ref[here, :].astype(F32) + dot(mixed_ref[here, :], wo_ref[...])
        residual_ref[here, :] = residual
        xhat, _ = normalise(residual)
        two = (xhat * gain_two[...] + shift_two[...]).astype(BF)
        two_ref[here, :] = two
        logits = dot(two, router_ref[...])
        valid = iota(logits.shape, 1) < experts
        logits = jnp.where(valid, logits, NEGATIVE)
        exponent = jnp.exp(logits - jnp.max(logits, axis=1, keepdims=True))
        soft = exponent / jnp.sum(exponent, axis=1, keepdims=True)
        soft_ref[here, :] = soft
        high, low = high_low(soft)
        side_ref[here, 0:128] = high
        side_ref[here, 128:256] = low
        return carry

    lax.fori_loop(0, rows // step, finish, 0)

    targets = row_ref[...]
    begin = 0
    for send_ref in (send_a, send_b):
        count = send_ref.shape[1]
        for e in range(experts):
            slot = iota((count, rows), 0) + (e * stride + begin)
            hit = (targets[0:1, :] == slot) | (targets[1:2, :] == slot)
            hot = jnp.where(hit, 1.0, 0.0).astype(BF)
            side = dot(hot, side_ref[...])
            side = side[:, 0:128] + side[:, 128:256]
            gate = jnp.sum(jnp.where(iota(side.shape, 1) == served(e, experts), side, 0.0), axis=1, keepdims=True)
            put_rows(send_ref, e, dot(hot, two_ref[...]), gate)
            if begin:
                send_ref[e, :, width:] = dot(hot, cot_ref[...]).astype(BF)
        begin += count


def expert_kernel(x_ref, *refs, begin):
    first_ref, weights, outs = refs[0], refs[1:-5], refs[-5:]
    back_ref, res_ref, act_ref, pre_ref, grad_ref = outs
    chunks, count, width = back_ref.shape
    if begin:
        x_ref, cot_ref = x_ref.at[:, :, 0:width], x_ref.at[:, :, width:]
        res_ref[:, 0:begin, :] = first_ref[...]
    else:
        cot_ref = first_ref
    units = weights[0].shape[0] // 2
    gate = jnp.concatenate([get_column(x_ref, c, width) for c in range(chunks)])
    x = x_ref[...].reshape(chunks * count, width)
    cot = cot_ref[...].reshape(chunks * count, width).astype(F32)
    grad = (gate * cot).astype(BF)
    grad_ref[...] = grad.reshape(chunks, count, width)
    for s, weight in enumerate(weights):
        cols = pl.ds(s * units, units)
        hidden = dot_nt(x, weight[0:units, :])
        below, bell = cumulative(hidden)
        act_ref[:, :, cols] = (hidden * below).astype(BF).reshape(chunks, count, units)
        pre = (dot_nt(grad, weight[units:, :]) * (below + hidden * bell)).astype(BF)
        pre_ref[:, :, cols] = pre.reshape(chunks, count, units)
    act = act_ref[...].reshape(chunks * count, -1)
    pre = pre_ref[...].reshape(chunks * count, -1)
    result = dot(act, jnp.concatenate([w[units:, :] for w in weights]))
    back = dot(pre, jnp.concatenate([w[0:units, :] for w in weights]))
    res_ref[:, begin : begin + count, :] = (gate * result).astype(BF).reshape(chunks, count, width)
    along = jnp.sum(cot * result, axis=1, keepdims=True)
    for c in range(chunks):
        here = slice(c * count, (c + 1) * count)
        put_rows(back_ref, c, back[here], along[here])


def first_grad_kernel(x_ref, pre_ref, act_ref, grad_ref, out_ref):
    units = pre_ref.shape[1]
    out_ref[0, 0:units, :] = dot_tn(pre_ref[...], x_ref[...]).astype(BF)
    out_ref[0, units:, :] = dot_tn(act_ref[...], grad_ref[...]).astype(BF)


def second_grad_kernel(x_ref, pre_ref, act_ref, grad_ref, first_ref, near_ref, far_in, far_out):
    units = pre_ref.shape[1]
    near = pl.program_id(0) < pl.num_programs(0) // 2
    grad_in = (dot_tn(pre_ref[...], x_ref[...]) + first_ref[0, 0:units, :].astype(F32)).astype(BF)
    grad_out = (dot_tn(act_ref[...], grad_ref[...]) + first_ref[0, units:, :].astype(F32)).astype(BF)

    @pl.when(near)
    def _():
        near_ref[0, 0:units, :] = grad_in
        near_ref[0, units:, :] = grad_out

    @pl.when(jnp.logical_not(near))
    def _():
        far_in[0] = grad_in
        far_out[0] = grad_out


def hot_of(col_ref, here, slots):
    columns = col_ref[here, :]
    slot = iota((columns.shape[0], slots), 1)
    hit = (columns[:, 0:1] == slot) | (columns[:, 1:2] == slot)
    return jnp.where(hit, 1.0, 0.0).astype(BF)


def combine_kernel(
    back_a, back_b, col_ref, soft_ref, residual_ref, cot_ref, two_ref, mixed_ref, gain_two, router_ref, wo_ref,
    resid_ref, gm_ref, wg_out_ref, wg_router_ref, small_ref, slots_ref, total_ref, *, experts, stride,
):
    at = pl.program_id(0)
    width = cot_ref.shape[1]

    @pl.when(at == 0)
    def _():
        for e in range(experts):
            base = e * stride
            for back_ref in (back_a, back_b):
                here = slice(base, base + back_ref.shape[1])
                base += back_ref.shape[1]
                slots_ref[here, 0:width] = back_ref[e]
                along = get_column(back_ref, e, width)
                label = iota((along.shape[0], 128), 1)
                high, low = high_low(jnp.where(label == served(e, experts), along, 0.0))
                slots_ref[here, width : width + 128] = high
                slots_ref[here, width + 128 : width + 256] = low
        small_ref[...] = jnp.zeros(small_ref.shape, F32)
        wg_router_ref[...] = jnp.zeros(wg_router_ref.shape, F32)
        total_ref[...] = jnp.zeros(total_ref.shape, F32)

    both = dot(hot_of(col_ref, slice(None), experts * stride), slots_ref[...])
    grad_two = both[:, 0:width]
    grad_gate = both[:, width : width + 128] + both[:, width + 128 : width + 256]
    soft = soft_ref[...]
    inner = jnp.sum(soft * grad_gate, axis=1, keepdims=True)
    logits = (soft * (grad_gate - inner)).astype(BF)
    grad_two = grad_two + dot_nt(logits, router_ref[...])
    xhat, rstd = normalise(residual_ref[...])
    grad = cot_ref[...].astype(F32) + norm_back(grad_two, xhat, rstd, gain_two[...])
    resid_ref[...] = grad
    low = grad.astype(BF)
    gm_ref[...] = dot_nt(low, wo_ref[...]).astype(BF)
    which = iota(small_ref.shape, 0)
    gain_sum = jnp.sum(grad_two * xhat, axis=0, keepdims=True)
    shift_sum = jnp.sum(grad_two, axis=0, keepdims=True)
    small_ref[...] += jnp.where(which == 0, gain_sum, jnp.where(which == 1, shift_sum, 0.0))
    wg_router_ref[...] += dot_tn(logits, two_ref[...])
    total_ref[...] += dot_tn(mixed_ref[...], low)

    @pl.when(at == pl.num_programs(0) - 1)
    def _():
        wg_out_ref[...] = total_ref[...].astype(BF)


def attention_back_kernel(
    side_ref, gm_ref, q_ref, k_ref, v_ref, prob_ref, normed_ref, wo_ref, gq_ref, gk_ref, gv_ref, near_ref,
    far_0, far_1, far_2, far_3, gq_all, gk_all, gv_all, *, group,
):
    patches, width = gm_ref.shape
    size = width // HEADS
    lanes = group * size
    here = pl.ds(pl.multiple_of(pl.program_id(0) * patches, 16), patches)
    for g in range(HEADS // group):
        cols = pl.ds(g * lanes, lanes)
        probs = prob_ref[0, g]
        wide = probs.astype(F32)
        mixed = stack_heads(gm_ref[:, cols], group, size)
        grad_probs = dot_nt(v_ref[:, cols], mixed)
        inner = jnp.sum(grad_probs * wide, axis=0, keepdims=True)
        scores = (wide * (grad_probs - inner)).astype(BF)
        queries = take_heads(dot_tn(scores, k_ref[:, cols]), group, size)
        for all_ref, one_ref, value in (
            (gv_all, gv_ref, dot(probs, mixed)),
            (gk_all, gk_ref, dot(scores, stack_heads(q_ref[:, cols], group, size))),
            (gq_all, gq_ref, queries * size**-0.5),
        ):
            low = value.astype(BF)
            all_ref[here, cols] = low
            one_ref[:, cols] = low

    @pl.when(pl.program_id(0) == pl.num_programs(0) - 1)
    def _():
        upper = side_ref[0] == 1
        lower = jnp.logical_not(upper)

        def put(n, value):
            @pl.when(upper if n // 2 else lower)
            def _():
                near_ref[n % 2] = value

            @pl.when(lower if n // 2 else upper)
            def _():
                for part, ref in enumerate(((far_0, far_1), (far_2, far_3))[n % 2]):
                    ref[...] = value[part * ref.shape[0] : (part + 1) * ref.shape[0]]

        put(0, wo_ref[...])
        for n, grad_ref in enumerate((gq_all, gk_all, gv_all)):
            put(n + 1, dot_tn(normed_ref[...], grad_ref[...]).astype(BF))


def output_kernel(col_ref, residual_ref, res_ref, out_ref):
    rows = residual_ref.shape[0]
    step = row_block(rows)

    def combine(block, carry):
        here = pl.ds(pl.multiple_of(block * step, 16), step)
        moe = dot(hot_of(col_ref, here, res_ref.shape[0]), res_ref[...])
        out_ref[here, :] = (residual_ref[here, :] + moe).astype(BF)
        return carry

    lax.fori_loop(0, rows // step, combine, 0)


def image_kernel(gq_ref, gk_ref, gv_ref, wq_ref, wk_ref, wv_ref, image_ref, resid_ref, gain_one, out_ref, small_ref):
    rows, width = image_ref.shape
    step = row_block(rows)

    def finish(block, carry):
        gain_sum, shift_sum = carry
        here = pl.ds(pl.multiple_of(block * step, 16), step)
        grad = dot_nt(gq_ref[here, :], wq_ref[...])
        grad = grad + dot_nt(gk_ref[here, :], wk_ref[...])
        grad = grad + dot_nt(gv_ref[here, :], wv_ref[...])
        xhat, rstd = normalise(image_ref[here, :].astype(F32))
        out_ref[here, :] = resid_ref[here, :] + norm_back(grad, xhat, rstd, gain_one[...])
        gain_sum = gain_sum + jnp.sum(grad * xhat, axis=0, keepdims=True)
        shift_sum = shift_sum + jnp.sum(grad, axis=0, keepdims=True)
        return gain_sum, shift_sum

    zero = jnp.zeros((1, width), F32)
    gain_sum, shift_sum = lax.fori_loop(0, rows // step, finish, (zero, zero))
    which = iota((8, width), 0)
    small_ref[...] = jnp.where(which == 0, gain_sum, jnp.where(which == 1, shift_sum, 0.0))


LENGTH = {
    "pack": 1,
    "route": 7,
    "forward": 19,
    "expert": 21,
    "first_grad": 9,
    "second_grad": 9,
    "combine": 17,
    "attention_back": 1,
    "output": 1,
    "image": 1,
}


def cost(name):
    length = LENGTH[name]
    return pl.CostEstimate(flops=int(length * 1.1e9), bytes_accessed=int(length * 3.4e6), transcendentals=0)


SCALAR = pl.BlockSpec(memory_space=pltpu.SMEM)
VECTOR = pl.BlockSpec(memory_space=pltpu.VMEM)


def call(kernel, outs, args, scalars=0, scratch=(), **names):
    return pl.pallas_call(
        functools.partial(kernel, **names) if names else kernel,
        out_shape=[jax.ShapeDtypeStruct(shape, kind) for shape, kind in outs],
        in_specs=[SCALAR] * scalars + [VECTOR] * (len(args) - scalars),
        out_specs=[VECTOR] * len(outs),
        scratch_shapes=scratch,
        compiler_params=pltpu.CompilerParams(vmem_limit_bytes=56 << 20),
        cost_estimate=cost(kernel.__name__.removesuffix("_kernel")),
        name=kernel.__name__,
    )(*args)


def make_on_device(experts, hidden):
    group = ("hh", "em", "el")
    half_h = hidden // 2
    places = [(eh, em, hh) for eh in range(2) for em in range(2) for hh in range(2)]

    def step(value, home, eh, hh):
        pairs = [
            (places.index(p), places.index((p[0] ^ eh, p[1], p[2] ^ hh)))
            for p in places
            if (p[0] == p[1] ^ p[2]) == home
        ]
        return lax.ppermute(value, ("eh", "em", "hh"), pairs)

    def over_hh(value):
        return swap(value, "hh", 2, 1)

    def with_three(value, axes, size):
        low, high = 1, size // 2
        one, two, three = (swap(value, axes, size, flip) for flip in (low, high, low | high))
        return (value + one) + (two + three)

    def over_eh(value):
        return swap(value, "eh", 2, 1)

    def fold_hl(parts):
        for bit in reversed(range(half_h.bit_length() - 2)):
            count = parts.shape[0] // 2
            far = swap(parts[count:], "hl", half_h, 1 << bit)
            parts = (parts[:count].astype(F32) + far.astype(F32)).astype(BF)
        return parts

    def gather_hl(parts, count):
        index = lax.axis_index("hl")
        for bit in range(count.bit_length() - 1):
            far = swap(parts, "hl", half_h, 1 << bit)
            odd = ((index >> bit) & 1) == 1
            parts = jnp.where(odd, jnp.concatenate([far, parts]), jnp.concatenate([parts, far]))
        return parts

    def scatter_hl(parts):
        index = lax.axis_index("hl")
        for bit in reversed(range(parts.shape[0].bit_length() - 1)):
            pairs = parts.reshape((2, -1) + parts.shape[1:])
            odd = (index >> bit) & 1
            keep = lax.dynamic_index_in_dim(pairs, odd, 0, keepdims=False)
            give = lax.dynamic_index_in_dim(pairs, 1 - odd, 0, keepdims=False)
            far = swap(give, "hl", half_h, 1 << bit)
            parts = (keep.astype(F32) + far.astype(F32)).astype(BF)
        return parts[0]

    def on_device(
        images,
        lengths,
        priority,
        top_experts,
        out_grad,
        first_gain,
        first_shift,
        w_query,
        w_key,
        w_value,
        w_output,
        second_gain,
        second_shift,
        w_router,
        w_expert_in,
        w_expert_out,
    ):
        devices = experts * hidden
        image_count, patches, width = images.shape
        rows = image_count * patches
        units = w_expert_in.shape[2]
        hidden_all = units * hidden
        capacity = (21 * rows * TOPK + 20 * experts - 1) // (20 * experts)
        stride = (capacity + 4 + 15) // 16 * 16
        count_a = stride // 2 // 16 * 16
        slots = experts * stride
        hh = lax.axis_index("hh")
        home = lax.axis_index("eh") == hh ^ lax.axis_index("em")

        block_a = ((experts, count_a, width), BF)
        block_b = ((experts, stride - count_a, 2 * width), BF)
        token_low = ((rows, width), BF)
        token_wide = ((rows, width), F32)

        (own,) = call(pack_kernel, [((2 * units, width), BF)], [w_expert_in[0], w_expert_out[0]])
        moved = [step(own, True, 1, 0), step(own, False, 0, 1), step(own, False, 1, 1)]

        cot = out_grad.reshape(rows, width)
        column, row, cot_a = call(
            route_kernel,
            [((rows, 128), I32), ((8, rows), I32), block_a],
            [lengths, priority, top_experts.reshape(rows, TOPK).T, cot],
            scalars=1,
            scratch=[pltpu.VMEM((rows, 128), F32), pltpu.VMEM((rows, rows), BF)],
            experts=experts,
            capacity=capacity,
            first=count_a - 2,
            stride=stride,
            patches=patches,
        )
        cot_a = to_all(cot_a, group)

        gain_one, shift_one, gain_two, shift_two = (
            v.reshape(1, width) for v in (first_gain, first_shift, second_gain, second_shift)
        )
        router = jnp.pad(w_router, ((0, 0), (0, 128 - experts)))
        tokens = images.reshape(rows, width)
        normed, queries, keys, values, probs, mixed, residual, two, soft, send_a, send_b = call(
            forward_kernel,
            [token_low] * 4
            + [((image_count, HEADS // GROUP, patches, GROUP * patches), BF), token_low, token_wide]
            + [token_low, ((rows, 128), F32), block_a, block_b],
            [lengths, tokens, cot, gain_one, shift_one, w_query, w_key, w_value, w_output]
            + [gain_two, shift_two, router, row],
            scalars=1,
            scratch=[pltpu.VMEM((rows, 256), BF)],
            experts=experts,
            stride=stride,
            patches=patches,
            group=GROUP,
        )

        send_a, cot_a, moved = together(send_a, cot_a, moved)
        x_a = to_all(send_a, group)
        by_eh, by_hh, by_both = moved
        weights = [jnp.where(home, own, by_eh), jnp.where(home, by_hh, by_both)]
        for bit in range(half_h.bit_length() - 1):
            weights = weights + [swap(w, "hl", half_h, 1 << bit) for w in weights]
        send_b, weights = together(send_b, weights)
        x_b = to_all(send_b, group)

        def serve(begin, *arrays):
            count = arrays[0].shape[1]

            def spec(rows_here, lanes):
                return pl.BlockSpec((2, rows_here, lanes), lambda i: (i, 0, 0))

            outs = [(count, n) for n in (width, width, hidden_all, hidden_all, width)]
            outs[1] = (begin + count, width)
            return pl.pallas_call(
                functools.partial(expert_kernel, begin=begin),
                grid=(experts // 2,),
                out_shape=[jax.ShapeDtypeStruct((experts,) + o, BF) for o in outs],
                in_specs=[spec(*a.shape[1:]) for a in arrays]
                + [pl.BlockSpec(w.shape, lambda i: (0, 0)) for w in weights],
                out_specs=[spec(*o) for o in outs],
                compiler_params=pltpu.CompilerParams(vmem_limit_bytes=56 << 20),
                cost_estimate=cost("expert"),
                name="expert_kernel",
            )(*arrays, *weights)

        half = hidden // 2

        def near(f):
            return (jnp.minimum(f, half - 1), 0, 0)

        def far(f):
            return (jnp.maximum(f - half, 0), 0, 0)

        def weight_grads(kernel, x, pre, act, grad, outs, *first):
            arrays = [a.reshape(-1, a.shape[2]) for a in (x, pre, act, grad)]
            count = arrays[0].shape[0]
            full = pl.BlockSpec((count, width), lambda f: (0, 0))
            part = pl.BlockSpec((count, units), lambda f: (0, f))
            piece = [pl.BlockSpec((1,) + a.shape[1:], lambda f: (f, 0, 0)) for a in first]
            return pl.pallas_call(
                kernel,
                grid=(hidden,),
                out_shape=[jax.ShapeDtypeStruct((n, rows_here, width), BF) for n, rows_here, _ in outs],
                in_specs=[full, part, part, full] + piece,
                out_specs=[pl.BlockSpec((1, rows_here, width), at) for _, rows_here, at in outs],
                compiler_params=pltpu.CompilerParams(vmem_limit_bytes=56 << 20),
                cost_estimate=cost(kernel.__name__.removesuffix("_kernel")),
                name=kernel.__name__,
            )(*arrays, *first)

        back_a, result, act_a, pre_a, grad_a = serve(0, x_a, cot_a)
        back_a = to_all(back_a, group)
        (first,) = weight_grads(
            first_grad_kernel, x_a, pre_a, act_a, grad_a, [(hidden, 2 * units, lambda f: (f, 0, 0))]
        )
        x_b, first = together(x_b, first)
        back_b, result, act_b, pre_b, grad_b = serve(count_a, x_b, result)
        back_a, back_b = together(back_a, back_b)
        back_b = to_all(back_b, group)
        back_b, result = together(back_b, result)
        result = to_all(result, group)
        outs = [(half, 2 * units, near), (half, units, far), (half, units, far)]
        grads_near, *grads_far = weight_grads(
            second_grad_kernel, x_b, pre_b, act_b, grad_b, outs, first
        )

        came = [swap(g, "hl", half_h, half_h // 2) for g in grads_far]
        came = jnp.concatenate(came, axis=1)
        parts = fold_hl((grads_near.astype(F32) + came.astype(F32)).astype(BF))
        cut = units * 44 // 32
        passed_one, passed_two = over_hh(parts[1, :cut]), over_hh(parts[1, cut:])

        def split(keep, passed):
            return jnp.where(home, keep, passed), jnp.where(home, passed, keep)

        def blocks_of(*arrays):
            step = row_block(rows)
            return [
                pl.BlockSpec((step, a.shape[1]), lambda i: (i, 0))
                if a.shape[0] == rows
                else pl.BlockSpec(a.shape, lambda i, n=len(a.shape): (0,) * n)
                for a in arrays
            ]

        arrays = [back_a, back_b, column, soft, residual, cot, two, mixed, gain_two, router, w_output]
        outs = [token_wide, token_low, ((width, width), BF), ((128, width), F32), ((8, width), F32)]
        outs = [jax.ShapeDtypeStruct(*o) for o in outs]
        resid, grad_mixed, wg_out, wg_router, small_two = pl.pallas_call(
            functools.partial(combine_kernel, experts=experts, stride=stride),
            grid=(rows // row_block(rows),),
            out_shape=outs,
            in_specs=blocks_of(*arrays),
            out_specs=blocks_of(*outs),
            scratch_shapes=[pltpu.VMEM((slots, width + 256), BF), pltpu.VMEM((width, width), F32)],
            compiler_params=pltpu.CompilerParams(vmem_limit_bytes=56 << 20),
            cost_estimate=cost("combine"),
            name="combine_kernel",
        )(*arrays)
        side = (lax.axis_index("hl") // (half_h // 2)).reshape(1)
        one = pl.BlockSpec((patches, width), lambda i: (i, 0))
        whole = pl.BlockSpec((rows, width), lambda i: (0, 0))
        square = pl.BlockSpec((width, width), lambda i: (0, 0))
        gq, gk, gv, wg_near, *wg_far = pl.pallas_call(
            functools.partial(attention_back_kernel, group=GROUP),
            grid=(image_count,),
            out_shape=[jax.ShapeDtypeStruct((rows, width), BF)] * 3
            + [jax.ShapeDtypeStruct((2, width, width), BF)]
            + [jax.ShapeDtypeStruct((width // 2, width), BF)] * 4,
            in_specs=[SCALAR, one, one, one, one]
            + [pl.BlockSpec((1,) + probs.shape[1:], lambda i: (i, 0, 0, 0)), whole, square],
            out_specs=[one] * 3 + [pl.BlockSpec((2, width, width), lambda i: (0, 0, 0))]
            + [pl.BlockSpec((width // 2, width), lambda i: (0, 0))] * 4,
            scratch_shapes=[pltpu.VMEM((rows, width), BF)] * 3,
            compiler_params=pltpu.CompilerParams(vmem_limit_bytes=56 << 20),
            cost_estimate=cost("attention_back"),
            name="attention_back_kernel",
        )(side, grad_mixed, queries, keys, values, probs, normed, wg_out)

        (block_out,) = call(
            output_kernel,
            [token_low],
            [column, residual, result.reshape(slots, width)],
        )
        grad_images, small_one = call(
            image_kernel,
            [token_wide, ((8, width), F32)],
            [gq, gk, gv, w_query, w_key, w_value, tokens, resid, gain_one],
        )

        small = jnp.concatenate([small_one[:2], small_two[:2], wg_router[:experts]])
        others = [swap(small, ("eh", "em"), 4, flip) for flip in (1, 2, 3)]
        others, block_out = together(others, block_out)
        small = (small + others[0]) + (others[1] + others[2])

        came = jnp.concatenate([swap(w, "hl", half_h, half_h // 2) for w in wg_far]).reshape(wg_near.shape)
        pieces = (wg_near.astype(F32) + came.astype(F32)).astype(BF)
        pieces = scatter_hl(pieces.reshape(half_h // 2, -1, width))
        pieces, passed_one = together(pieces, passed_one)
        pieces = to_all(pieces.reshape(experts, -1, width), group)
        mine_one, theirs_one = split(parts[0, :cut], passed_one)
        far_one = over_eh(theirs_one)
        pieces, far_one, passed_two, block_out, grad_images, small = together(
            pieces, far_one, passed_two, block_out, grad_images, small
        )
        mine_two, theirs_two = split(parts[0, cut:], passed_two)
        far_two = over_eh(theirs_two)
        piece = jnp.sum(pieces.astype(F32), axis=0)
        piece = (piece + over_eh(piece.astype(BF)).astype(F32)).astype(BF)
        pieces = to_all(jnp.broadcast_to(piece, (experts,) + piece.shape), group)
        sums = [mine_one.astype(F32) + far_one.astype(F32), mine_two.astype(F32) + far_two.astype(F32)]
        sums = jnp.concatenate(sums)
        sum_in, sum_out = sums[:units].T, sums[units:]
        for bit in range(half_h.bit_length() - 1):
            small = small + swap(small, "hl", half_h, 1 << bit)
        for bit in range((experts // 8).bit_length() - 1):
            small = small + swap(small, "el", experts // 4, 1 << bit)
        small = with_three(small, ("el", "hh"), experts // 2)
        pieces, small, sum_in, sum_out = together(pieces, small, sum_in, sum_out)
        pieces = gather_hl(pieces.reshape(1, -1, width), half_h // 2)
        came = swap(pieces, "hl", half_h, half_h // 2)
        lower = jnp.where(side[0] == 0, pieces, came).reshape(2, width, width).astype(F32)
        upper = jnp.where(side[0] == 0, came, pieces).reshape(2, width, width).astype(F32)
        return (
            block_out.reshape(images.shape),
            grad_images.reshape(images.shape),
            small[0],
            small[1],
            lower[1],
            upper[0],
            upper[1],
            lower[0],
            small[2],
            small[3],
            small[4:].T,
            sum_in[None],
            sum_out[None],
        )

    return on_device


def solution(mesh):
    experts, hidden = mesh.shape["expert"], mesh.shape["hidden"]
    names = ("eh", "em", "el", "hh", "hl")
    places = mesh.devices.reshape(2, 2, experts // 4, 2, hidden // 2)
    tokens = (P(names, None, None), P(names), P(names, None), P(names, None, None), P(names, None, None))
    weights = (P(names[:3], None, names[3:]), P(names[:3], names[3:], None))
    return jax.shard_map(
        make_on_device(experts, hidden),
        mesh=jax.sharding.Mesh(places, names),
        in_specs=tokens + (P(),) * 9 + weights,
        out_specs=(P(names, None, None),) * 2 + (P(),) * 9 + weights,
        check_vma=False,
    )
```
